128 devices in a mesh: comp: 4 (over z), blk: 32 (over x, y, core).
Axes of the slice: x: 4, y: 4, z: 4, core: 2. Of those that a mesh axis runs over, the one named last changes fastest.
Arguments:
- adjoint: bfloat16 [524288, 320], P(('comp', 'blk')), may hold values from -6 to 6
- metric: bfloat16 [524288, 320], P(('comp', 'blk')), may hold values from 0.099609375 to 1.8984375
- comp_jac: bfloat16 [4, 320, 320], P('comp'), may hold values from -0.3125 to 0.3125
- face_jac: bfloat16 [320, 320], replicated, may hold values from -0.3125 to 0.3125
- donor_weights: bfloat16 [2, 320, 320], replicated, may hold values from -0.3125 to 0.3125
- source: bfloat16 [524288, 320], P(('comp', 'blk')), may hold values from -18 to 18
- face_nbr: int32 [49152], P(('comp', 'blk')), may hold values from 0 to 1535
- receiver_block: int32 [262144], P(('comp', 'blk')), may hold values from 0 to 4095
- donor_owner: int32 [262144, 1], P(('comp', 'blk')), may hold values from 0 to 127; in each aligned block of 2048 rows (0 to 2047, 2048 to 4095, ...) at most 24 rows name the same one
- donor_block: int32 [262144], P(('comp', 'blk')), may hold values from 0 to 4095
- donor_slot: int32 [262144], P(('comp', 'blk')), may hold values from 0 to 1
- fringe_count: int32 [128], P(('comp', 'blk')), may hold values from 512 to 2048, as said below
Outputs:
- adjoint_residual: bfloat16 [524288, 320], P(('comp', 'blk'))
- imbalance: float32 [], replicated
The draws below stay inside these ranges and needn't reach their ends.
Inputs may be any that keep to these rules, and one draw needn't show every extreme that they name: `donor_owner`: within the records of one device (aligned blocks of 2048 rows) no device is named more than 24 times, and some device is named exactly 24 times. `fringe_count`: some device has all 2048 records live.
All inputs are finite; a program needn't handle non-finite values.
Results may differ from the reference program's by a relative error of at most 0.0055.
Values may be sent and summed in bfloat16 or wider, within the bound.
No kernel may reach another device: no remote copies, remote signals or barrier semaphores. Data moves between devices by JAX's collectives and lax.ppermute only.
A program may use at most 128 MiB of HBM per device.

```python
import math
import jax
import jax.numpy as jnp
import numpy as np
from jax import lax

NODES = 64
W = 320
SLOTS = 2
BLK_DEV = 4096
IFB = 384
FR_DEV = 2048
CAP = 24
BLOCKS = 524288
IFACES = 49152
RECORDS = 262144
N_COMP = 4
N_BLK = 32


def draw_source(key, part):
    key = jax.random.fold_in(key, 7)
    rows = jnp.arange(BLOCKS, dtype=jnp.float32)[:, None] / (BLOCKS - 1)
    base = jnp.clip(jax.random.normal(key, (BLOCKS, W), jnp.float32), -6.0, 6.0)
    spread = 1.0 + 2.0 * rows
    return jnp.clip(base * spread, -18.0, 18.0).astype(jnp.bfloat16)


def draw_fringe_count(key, part):
    key = jax.random.fold_in(key, 11)
    first, second = jax.random.split(key)
    count_all = N_COMP * N_BLK
    counts = jax.random.randint(first, (count_all,), FR_DEV // 4, FR_DEV + 1)
    full = jax.random.randint(second, (), 0, count_all)
    return jnp.where(jnp.arange(count_all) == full, FR_DEV, counts).astype(jnp.int32)


def place_ends(array, rng, low, top_value):
    extent = array.shape
    index_at = [jax.random.randint(jax.random.fold_in(rng, axis), (), 0, extent[axis]) for axis in range(len(extent))]
    array = array.at[tuple(index_at)].set(low)
    longest = extent.index(max(extent))
    index_at[longest] = (index_at[longest] + 1) % extent[longest]
    return array.at[tuple(index_at)].set(top_value)


def block_levels(key, dims, cuts, least, top_value):
    loudness, own = 1.0, jax.random.fold_in(key, 6)
    for axis_at, blocks in cuts:
        steps = jnp.exp(jax.random.uniform(jax.random.fold_in(own, axis_at), (blocks,), jnp.float32, least / len(cuts), top_value / len(cuts)))
        loudness = loudness * jnp.repeat(steps, dims[axis_at] // blocks).reshape([-1 if axis == axis_at else 1 for axis in range(len(dims))])
    return loudness


def shared_out(key, own, number, rows, amount, top, most, skew):
    order = jax.random.permutation(key, amount)
    heavy_load, ordinary = shares(amount, rows * top, most, skew, True), shares(amount, rows * top, most, skew, False)
    places = jnp.arange(amount)

    def named(tallies, offset_by):
        used = int((tallies > 0).sum())
        fixed = max(1, used // 4)
        shifted = fixed + (places - fixed + offset_by * (used - fixed)) % max(1, amount - fixed)
        return jnp.zeros((amount,), jnp.int32).at[order[jnp.where(places < fixed, places, shifted)]].set(jnp.asarray(tallies, jnp.int32))

    tallies = jnp.where(number % 4 == 0, named(heavy_load, number // 4), named(ordinary, number - number // 4 - 1))
    mixed = jax.random.permutation(jax.random.fold_in(own, 3), amount)
    source_of, receiver = mixed[0:amount // 2 * 2:2], mixed[1:amount // 2 * 2:2]
    margin = jnp.minimum(tallies[source_of] - 1, most - tallies[receiver]) // 2
    margin = jnp.where((source_of == order[0]) | (receiver == order[0]) | (tallies[receiver] == 0), 0, jnp.maximum(margin, 0))
    shifted = jax.random.randint(jax.random.fold_in(own, 4), (amount // 2,), 0, 1 << 20) % (margin + 1)
    tallies = tallies.at[source_of].add(-shifted).at[receiver].add(shifted)
    members = jnp.searchsorted(jnp.cumsum(tallies), jnp.arange(rows * top), side="right").astype(jnp.int32)
    grid = members.reshape(top, rows).T
    grid = grid[jax.random.permutation(jax.random.fold_in(own, 1), rows)]
    offset_by = jax.random.randint(jax.random.fold_in(own, 2), (rows, 1), 0, top)
    return jnp.take_along_axis(grid, (jnp.arange(top)[None, :] + offset_by) % top, axis=1)


def shares(count, total, limit, lean, full):
    portions = [(1 << 20) // math.isqrt(grade ** lean) + 1 for grade in range(1, count + 1)]
    largest = limit if full else min(limit, max(-(-total // count), total * portions[0] // sum(portions)))
    least = 1 if total - largest >= count - 1 else 0
    holding, spare = [largest] + [least] * (count - 1), total - largest - least * (count - 1)
    while spare > 0:
        free = [i for i in range(1, count) if holding[i] < largest] or [i for i in range(1, count) if holding[i] < limit]
        mass, budget = sum([portions[i] for i in free]), spare
        for i in free:
            addition = min(limit - holding[i], max(1, budget * portions[i] // mass), spare)
            holding[i] = holding[i] + addition
            spare = spare - addition
    return np.array(holding)


def scatter_about(key, extent, deviation, limit, cuts=(), kind=jnp.bfloat16):
    drawn = deviation * jax.random.normal(key, extent, jnp.float32)
    if cuts:
        drawn = drawn * block_levels(key, extent, cuts, -0.22, 0.18)
    return jnp.clip(drawn, -limit, limit).astype(kind)


def setup_inputs(seed: int = 0) -> dict:
    keys = jax.random.split(jax.random.key(seed), 13)
    adjoint = scatter_about(keys[0], (BLOCKS, W), 1.0, 6.0, ((0, 128),))
    metric = jnp.clip(1.0 + 0.18 * jax.random.normal(keys[1], (BLOCKS, W), jnp.float32), 0.099609375, 1.8984375).astype(jnp.bfloat16)
    comp_jac = scatter_about(keys[2], (N_COMP, W, W), W ** -0.5, 0.3125, ((0, 4),))
    face_jac = scatter_about(keys[3], (W, W), W ** -0.5, 0.3125)
    donor_weights = scatter_about(keys[4], (SLOTS, W, W), W ** -0.5, 0.3125)
    source = draw_source(jax.random.fold_in(keys[12], 71), 0)
    face_nbr = place_ends(jax.random.randint(keys[6], (IFACES,), 0, N_COMP * IFB), jax.random.fold_in(keys[6], 1), 0, (N_COMP * IFB) - 1).astype(jnp.int32)
    receiver_block = place_ends(jax.random.randint(keys[7], (RECORDS,), 0, BLK_DEV), jax.random.fold_in(keys[7], 1), 0, BLK_DEV - 1).astype(jnp.int32)
    donor_owner_keys = jax.random.split(jax.random.fold_in(keys[8], 1), RECORDS // FR_DEV)
    donor_owner_turns = jax.random.permutation(jax.random.fold_in(keys[8], 3), RECORDS // FR_DEV)
    donor_owner = jax.vmap(lambda own, number: shared_out(jax.random.fold_in(keys[8], 2), own, number, FR_DEV, N_COMP * N_BLK, 1, CAP, 2))(donor_owner_keys, donor_owner_turns).reshape((RECORDS, 1))
    donor_block = place_ends(jax.random.randint(keys[9], (RECORDS,), 0, BLK_DEV), jax.random.fold_in(keys[9], 1), 0, BLK_DEV - 1).astype(jnp.int32)
    donor_slot = place_ends(jax.random.randint(keys[10], (RECORDS,), 0, SLOTS), jax.random.fold_in(keys[10], 1), 0, SLOTS - 1).astype(jnp.int32)
    fringe_count = draw_fringe_count(jax.random.fold_in(keys[12], 71), 0)
    return {"adjoint": adjoint, "metric": metric, "comp_jac": comp_jac, "face_jac": face_jac, "donor_weights": donor_weights, "source": source, "face_nbr": face_nbr, "receiver_block": receiver_block, "donor_owner": donor_owner, "donor_block": donor_block, "donor_slot": donor_slot, "fringe_count": fringe_count}


def reference(adjoint, metric, comp_jac, face_jac, donor_weights, source, face_nbr, receiver_block, donor_owner, donor_block, donor_slot, fringe_count):
    scaled = (adjoint.astype(jnp.float32) * metric.astype(jnp.float32)).astype(jnp.bfloat16)
    group = N_BLK * BLK_DEV
    pieces = []
    for comp_index in range(N_COMP):
        rows = scaled[comp_index * group:(comp_index + 1) * group]
        pieces.append(jnp.dot(rows, comp_jac[comp_index], preferred_element_type=jnp.float32))
    volume = jnp.concatenate(pieces, axis=0)
    face_ids = jnp.arange(IFACES, dtype=jnp.int32)
    face_dev = face_ids // IFB
    face_k = face_dev % N_BLK
    face_rows = face_dev * BLK_DEV + face_ids % IFB
    face_terms = jnp.dot(scaled[face_rows], face_jac, preferred_element_type=jnp.float32)
    face_target = (face_nbr // IFB * N_BLK + face_k) * BLK_DEV + face_nbr % IFB
    faces = jax.ops.segment_sum(face_terms, face_target, num_segments=BLOCKS)
    rec_ids = jnp.arange(RECORDS, dtype=jnp.int32)
    rec_dev = rec_ids // FR_DEV
    live = rec_ids % FR_DEV < fringe_count[rec_dev]
    records = scaled[rec_dev * BLK_DEV + receiver_block]
    wide_weights = jnp.transpose(donor_weights, (1, 0, 2)).reshape(W, SLOTS * W)
    wide = jnp.dot(records, wide_weights, preferred_element_type=jnp.float32).reshape(RECORDS, SLOTS, W)
    pick = lax.optimization_barrier(jnp.sum(jnp.where(donor_slot[:, None, None] == jnp.arange(SLOTS, dtype=jnp.int32)[None, :, None], wide, jnp.float32(0.0)), axis=1))
    contrib = jnp.where(live[:, None], pick.astype(jnp.bfloat16), jnp.zeros_like(pick, dtype=jnp.bfloat16))
    target = donor_owner[:, 0] * BLK_DEV + donor_block
    fringe = jax.ops.segment_sum(contrib.astype(jnp.float32), target, num_segments=BLOCKS)
    total = volume + faces + fringe - source.astype(jnp.float32)
    imbalance = jnp.sum(total[:, :NODES]) / jnp.sqrt(jnp.float32(BLOCKS * NODES))
    return (total.astype(jnp.bfloat16), imbalance)
```

```python
import functools

import jax
import jax.numpy as jnp
from jax import lax
from jax.experimental import pallas as pl
from jax.experimental.pallas import tpu as pltpu
from jax.sharding import PartitionSpec as P

NODES = 64
CAP = 24
LANES = 128
DOT00 = (((0,), (0,)), ((), ()))
DOT11 = (((1,), (1,)), ((), ()))
DOT10 = (((1,), (0,)), ((), ()))
F32 = jnp.float32
BF16 = jnp.bfloat16
VMEM_LIMIT = 60 * 1024 * 1024


def dot(a, b, dims):
    return lax.dot_general(a, b, dims, preferred_element_type=F32)


def iota(shape, axis):
    return lax.broadcasted_iota(jnp.int32, shape, axis)


def product(a, b):
    return (a.astype(F32) * b.astype(F32)).astype(BF16)


def pack_kernel(
    tiles, width, cnt_ref, owner_ref, recv_ref, slot_ref, dblk_ref, adj_ref, met_ref, src_ref, jac_ref, face_ref, w_ref,
    send_ref, wcat, rows, out_rows, code_v, code_s, numbers, sums, sem,
):
    t = pl.program_id(0)
    tile = adj_ref.shape[1]
    n_dev = send_ref.shape[0]
    n_rec = owner_ref.shape[1]
    slots = n_dev * CAP
    ifb = 384

    @pl.when(t == 0)
    def _():
        wcat[:, 0:256] = w_ref[0, :, 0:256]
        wcat[:, 256:512] = w_ref[1, :, 0:256]
        wcat[:, 512:640] = jnp.concatenate([w_ref[0, :, 256:320], w_ref[1, :, 256:320]], axis=1)
        sums[...] = jnp.zeros_like(sums)
        step = 256
        upper = (iota((step, step), 0) < iota((step, step), 1)).astype(BF16)
        j = iota((LANES, step), 0)
        krow = jnp.where(j < 64, -1, jnp.where(j < 88, j - 64, jnp.where(j < 112, j - 88, -1)))
        carry = jnp.zeros((n_dev, 1), F32)
        table = jnp.zeros((n_dev, LANES), F32)
        for c in range(n_rec // step):
            at = slice(c * step, (c + 1) * step)
            own = owner_ref[:, at]
            live = (iota((1, step), 1) + c * step) < cnt_ref[0]
            hit = (iota((n_dev, step), 0) == own) & live
            a = jnp.where(hit, 1.0, 0.0).astype(F32)
            ab = a.astype(BF16)
            before = dot(ab, upper, DOT10) + carry
            rank = jnp.sum(a * before, axis=0, keepdims=True).astype(jnp.int32)
            carry = carry + jnp.sum(a, axis=1, keepdims=True)
            place = jnp.where(live, own * CAP + rank, slots)
            code_v[:, at] = place * 8192 + recv_ref[:, at] * 2 + slot_ref[:, at]
            tag = dblk_ref[:, at] + 1
            feature = jnp.where(j < 88, tag >> 5, tag & 31)
            z = jnp.where(krow == rank, feature, 0).astype(F32).astype(BF16)
            table = table + dot(ab, z, DOT11)
        numbers[...] = table
        copy = pltpu.make_async_copy(code_v, code_s, sem)
        copy.start()
        out_rows[...] = jnp.zeros_like(out_rows)
        copy.wait()

    x = product(adj_ref[...], met_ref[...])
    y = dot(x, wcat[...], DOT00)
    base = t * tile * 8
    p2 = y[:, 512:640]
    for k, piece in ((0, y[:, 0:128]), (1, y[:, 128:256]), (2, p2), (4, y[:, 256:384]), (5, y[:, 384:512]), (6, pltpu.roll(p2, 64, 1))):
        rows[pl.ds(base + k, tile, stride=8), :] = piece
    xf = x.astype(F32)
    face_lane = iota((1, tile), 1) + t * tile < ifb
    sums[:, 0:1] += jnp.sum(xf, axis=1, keepdims=True)
    sums[:, 1:2] += jnp.sum(jnp.where(face_lane, xf, 0.0), axis=1, keepdims=True)
    sums[0:64, 2:3] += jnp.sum(src_ref[...].astype(F32), axis=1, keepdims=True)

    @pl.when(t == tiles - 1)
    def _():
        unroll = 8

        def move(i, _):
            for u in range(unroll):
                code = code_s[0, i * unroll + u]
                to = pl.multiple_of((code >> 13) * 4, 4)
                at = pl.multiple_of((code & 8191) * 4, 4)
                out_rows[pl.ds(to, 4), :] = rows[pl.ds(at, 4), :]
            return 0

        lax.fori_loop(0, (cnt_ref[0] + unroll - 1) // unroll, move, 0)

        lane8 = iota((8, LANES), 1)

        def pieces(d):
            at = d * (CAP * 4)
            return [out_rows[pl.ds(at + k, CAP, stride=4), :] for k in range(3)]

        def total_q(d, acc):
            p0 = pieces(d)[0].astype(BF16).astype(F32)
            return acc + p0[0:8] + p0[8:16] + p0[16:24]

        jsum = jnp.sum(jac_ref[0, :, 0:NODES].astype(F32), axis=1, keepdims=True)
        fsum = jnp.sum(face_ref[:, 0:NODES].astype(F32), axis=1, keepdims=True)
        qsum = lax.fori_loop(0, n_dev, total_q, jnp.zeros((8, LANES), F32), unroll=8)
        mass = (
            jnp.sum(jnp.where(lane8 < NODES, qsum, 0.0), keepdims=True)
            + jnp.sum(sums[:, 0:1] * jsum + sums[:, 1:2] * fsum, keepdims=True)
            - jnp.sum(sums[0:64, 2:3], keepdims=True)
        )
        m0 = mass.astype(BF16).astype(F32)
        m1 = (mass - m0).astype(BF16).astype(F32)
        m2 = mass - m0 - m1
        lane = iota((n_dev, LANES), 1)
        numbers[...] += jnp.where(lane == 112, m0, jnp.where(lane == 113, m1, jnp.where(lane == 114, m2, 0.0)))

        def emit(d, _):
            p0, p1, p2 = pieces(d)
            low = jnp.where(lane8 < 64, p2[0:8], pltpu.roll(p2[16:24], 64, 1))
            high = jnp.where(lane8 < 64, p2[8:16], jnp.broadcast_to(numbers[pl.ds(d, 1), :], (8, LANES)))
            block = jnp.concatenate([p0[0:16], p1[0:16], p0[16:24], p1[16:24], low, high], axis=0)
            send_ref[d] = block.astype(BF16)
            return 0

        lax.fori_loop(0, n_dev, emit, 0, unroll=4)


def pack(cnt, owner, recv, slot, dblk, adj, met, src, jac, face, weights, n_dev):
    width, blocks = adj.shape
    n_rec = owner.shape[1]
    tile = 512
    tiles = blocks // tile
    col = lambda t: (0, t)
    fixed2 = lambda t: (0, 0)
    ints = pl.BlockSpec((1, n_rec), fixed2)
    return pl.pallas_call(
        functools.partial(pack_kernel, tiles, width),
        grid=(tiles,),
        in_specs=[
            pl.BlockSpec(memory_space=pltpu.SMEM),
            ints, ints, ints, ints,
            pl.BlockSpec((width, tile), col),
            pl.BlockSpec((width, tile), col),
            pl.BlockSpec((64, tile), col),
            pl.BlockSpec((1, width, width), lambda t: (0, 0, 0)),
            pl.BlockSpec((width, width), fixed2),
            pl.BlockSpec((2, width, width), lambda t: (0, 0, 0)),
        ],
        out_specs=pl.BlockSpec((n_dev, 64, LANES), lambda t: (0, 0, 0)),
        out_shape=jax.ShapeDtypeStruct((n_dev, 64, LANES), BF16),
        scratch_shapes=[
            pltpu.VMEM((width, 640), BF16),
            pltpu.VMEM((blocks * 8, LANES), F32),
            pltpu.VMEM((n_dev * CAP * 4 + 8, LANES), F32),
            pltpu.VMEM((1, n_rec), jnp.int32),
            pltpu.SMEM((1, n_rec), jnp.int32),
            pltpu.VMEM((n_dev, LANES), F32),
            pltpu.VMEM((width, LANES), F32),
            pltpu.SemaphoreType.DMA,
        ],
        compiler_params=pltpu.CompilerParams(vmem_limit_bytes=VMEM_LIMIT),
        cost_estimate=pl.CostEstimate(flops=2 * blocks * width * 2 * width, bytes_accessed=8 << 20, transcendentals=0),
        name="pack",
    )(cnt, owner, recv, slot, dblk, adj, met, src, jac, face, weights)


def face_out_kernel(adj_ref, met_ref, nbr_ref, out_ref):
    width, ifb = adj_ref.shape
    out_ref[0:width, :] = product(adj_ref[...], met_ref[...])
    nbr = nbr_ref[...]
    r = iota((16, ifb), 0)
    out_ref[width:width + 16, :] = jnp.where(r < 8, nbr >> 5, nbr & 31).astype(F32).astype(BF16)


def face_out(adj, met, nbr):
    width, _ = adj.shape
    ifb = nbr.shape[1]
    return pl.pallas_call(
        face_out_kernel,
        grid=(1,),
        in_specs=[
            pl.BlockSpec((width, ifb), lambda t: (0, 0)),
            pl.BlockSpec((width, ifb), lambda t: (0, 0)),
            pl.BlockSpec((1, ifb), lambda t: (0, 0)),
        ],
        out_specs=pl.BlockSpec((width + 16, ifb), lambda t: (0, 0)),
        out_shape=jax.ShapeDtypeStruct((width + 16, ifb), BF16),
        name="face_out",
    )(adj, met, nbr)


def partial_kernel(me_ref, adj_ref, met_ref, src_ref, jac_ref, face_ref, got_ref, out_ref):
    t = pl.program_id(0)
    width = adj_ref.shape[0]
    x = product(adj_ref[...], met_ref[...])
    out_ref[...] = dot(jac_ref[0], x, DOT00) - src_ref[...].astype(F32)

    @pl.when(t == 0)
    def _():
        n_comp = got_ref.shape[0] // (width + 16)
        ifb = got_ref.shape[1]
        acc = jnp.zeros((width, ifb), F32)
        for c in range(n_comp):
            at = c * (width + 16)
            term = dot(face_ref[...], got_ref[at:at + width, :], DOT00)
            number = got_ref[at + width:at + width + 16, :].astype(F32)
            nbr = (number[0:1] * 32.0 + number[8:9]).astype(jnp.int32) - me_ref[0] * ifb
            hit = jnp.where(iota((ifb, ifb), 0) == nbr, 1.0, 0.0).astype(F32).astype(BF16)
            acc = acc + dot(term.astype(BF16), hit, DOT11)
        out_ref[:, 0:ifb] += acc


def partial_total(me, adj, met, src, jac, face, got):
    width, blocks = adj.shape
    tile = 512
    col = lambda t: (0, t)
    return pl.pallas_call(
        partial_kernel,
        grid=(blocks // tile,),
        in_specs=[
            pl.BlockSpec(memory_space=pltpu.SMEM),
            pl.BlockSpec((width, tile), col),
            pl.BlockSpec((width, tile), col),
            pl.BlockSpec((width, tile), col),
            pl.BlockSpec((1, width, width), lambda t: (0, 0, 0)),
            pl.BlockSpec((width, width), lambda t: (0, 0)),
            pl.BlockSpec(got.shape, lambda t: (0, 0)),
        ],
        out_specs=pl.BlockSpec((width, tile), col),
        out_shape=jax.ShapeDtypeStruct((width, blocks), F32),
        compiler_params=pltpu.CompilerParams(vmem_limit_bytes=VMEM_LIMIT),
        cost_estimate=pl.CostEstimate(flops=2 * blocks * width * width, bytes_accessed=13 << 20, transcendentals=0),
        name="partial",
    )(me, adj, met, src, jac, face, got)


def unpack_kernel(scale, got_ref, part_ref, out_ref, mass_ref, q_t, index, q, numbers, hit):
    t = pl.program_id(0)
    n_dev = got_ref.shape[0]
    slots = n_dev * CAP
    width, tile = out_ref.shape

    @pl.when(t == 0)
    def _():
        def take(s, _):
            g = got_ref[s].astype(F32)
            at = pl.multiple_of(s * CAP, 8)
            q[pl.ds(at, 16), 0:128] = g[0:16]
            q[pl.ds(at, 16), 128:256] = g[16:32]
            q[pl.ds(at + 16, 8), 0:128] = g[32:40]
            q[pl.ds(at + 16, 8), 128:256] = g[40:48]
            q[pl.ds(at, 16), 256:384] = g[48:64]
            q[pl.ds(at + 16, 8), 256:384] = pltpu.roll(g[48:56], 64, 1)
            numbers[pl.ds(s, 1), :] = g[56:57]
            return 0

        lax.fori_loop(0, n_dev, take, 0, unroll=4)
        step = 256
        for c in range(slots // step):
            at = slice(c * step, (c + 1) * step)
            q_t[:, at] = q[at, :].T[0:width].astype(BF16)
        nums = numbers[...]
        lane = iota((n_dev, LANES), 1)
        mass_ref[0, 0] = jnp.sum(jnp.where((lane >= 112) & (lane < 115), nums, 0.0)) * scale
        nums = nums.astype(BF16)
        part = 16 * CAP
        row = iota((part, LANES), 0)
        lane = iota((part, LANES), 1)
        k = row % CAP
        pick = jnp.where(lane - 64 == k, 32.0, jnp.where(lane - 88 == k, 1.0, 0.0)).astype(F32)
        for c in range(n_dev // 16):
            source = jnp.where(lane == row // CAP + 16 * c, 1.0, 0.0).astype(F32).astype(BF16)
            value = jnp.sum(dot(source, nums, DOT10) * pick, axis=1, keepdims=True)
            index[c * part:(c + 1) * part, :] = jnp.broadcast_to(value.astype(jnp.int32) - 1, (part, LANES))

    lane = iota((256, LANES), 1)
    for c in range(slots // 256):
        at = slice(c * 256, (c + 1) * 256)
        ids = index[at, :] - t * tile
        for n in range(tile // LANES):
            hit[at, n * LANES:(n + 1) * LANES] = jnp.where(ids == lane + n * LANES, 1.0, 0.0).astype(F32).astype(BF16)
    out_ref[...] = (part_ref[...] + dot(q_t[...], hit[...], DOT10)).astype(BF16)


def unpack(got, part, scale):
    width, blocks = part.shape
    n_dev = got.shape[0]
    tile = 256
    slots = n_dev * CAP
    return pl.pallas_call(
        functools.partial(unpack_kernel, scale),
        grid=(blocks // tile,),
        in_specs=[
            pl.BlockSpec(got.shape, lambda t: (0, 0, 0)),
            pl.BlockSpec((width, tile), lambda t: (0, t)),
        ],
        out_specs=[
            pl.BlockSpec((width, tile), lambda t: (0, t)),
            pl.BlockSpec(memory_space=pltpu.SMEM),
        ],
        out_shape=[
            jax.ShapeDtypeStruct((width, blocks), BF16),
            jax.ShapeDtypeStruct((1, 1), F32),
        ],
        scratch_shapes=[
            pltpu.VMEM((width, slots), BF16),
            pltpu.VMEM((slots, LANES), jnp.int32),
            pltpu.VMEM((slots, 384), F32),
            pltpu.VMEM((n_dev, LANES), F32),
            pltpu.VMEM((slots, tile), BF16),
        ],
        compiler_params=pltpu.CompilerParams(vmem_limit_bytes=VMEM_LIMIT),
        cost_estimate=pl.CostEstimate(flops=2 * blocks * slots * width, bytes_accessed=10 << 20, transcendentals=0),
        name="unpack",
    )(got, part)


def shards(
    adjoint, metric, comp_jac, face_jac, donor_weights, source, face_nbr,
    receiver_block, donor_owner, donor_block, donor_slot, fringe_count,
):
    blocks, width = adjoint.shape
    n_dev = lax.axis_size("comp") * lax.axis_size("blk")
    adj, met, src = adjoint.T, metric.T, source.T
    row = lambda a: a.reshape(1, -1)
    faces = lax.all_gather(face_out(adj, met, row(face_nbr)), "comp", axis=0, tiled=True)
    send = pack(
        fringe_count, row(donor_owner), row(receiver_block), row(donor_slot), row(donor_block),
        adj, met, src, comp_jac, face_jac, donor_weights, n_dev,
    )
    got = lax.all_to_all(send, ("comp", "blk"), split_axis=0, concat_axis=0, tiled=True)
    me = lax.axis_index("comp").astype(jnp.int32).reshape(1)
    part = partial_total(me, adj, met, src, comp_jac, face_jac, faces)
    out, mass = unpack(got, part, 1.0 / float(blocks * n_dev * NODES) ** 0.5)
    return out.T, mass.reshape(())


def solution(mesh):
    both = ("comp", "blk")
    placed = (
        P(both, None), P(both, None), P("comp", None, None), P(), P(), P(both, None),
        P(both), P(both), P(both, None), P(both), P(both), P(both),
    )
    return jax.shard_map(
        shards, mesh=mesh, in_specs=placed, out_specs=(P(both, None), P()), check_vma=False,
    )
```

```python
import functools

import jax
import jax.numpy as jnp
from jax import lax
from jax.experimental import pallas as pl
from jax.experimental.pallas import tpu as pltpu
from jax.sharding import PartitionSpec as P

NODES = 64
CAP = 24
LANES = 128
DOT00 = (((0,), (0,)), ((), ()))
DOT11 = (((1,), (1,)), ((), ()))
DOT10 = (((1,), (0,)), ((), ()))
F32 = jnp.float32
BF16 = jnp.bfloat16
VMEM_LIMIT = 60 * 1024 * 1024


def dot(a, b, dims):
    return lax.dot_general(a, b, dims, preferred_element_type=F32)


def iota(shape, axis):
    return lax.broadcasted_iota(jnp.int32, shape, axis)


def product(a, b):
    return (a.astype(F32) * b.astype(F32)).astype(BF16)


def pack_kernel(
    tiles, ifb, cnt_ref, owner_ref, recv_ref, slot_ref, dblk_ref, adj_hbm, met_hbm, src_hbm, jac_hbm, face_hbm, w_hbm,
    send_ref, adj, met, src, jac, face, w, wcat, rows, stage, place_v, place_s, numbers, sems, late_sems, sem,
):
    n_dev = send_ref.shape[0]
    n_rec = owner_ref.shape[1]

    w_copy = pltpu.make_async_copy(w_hbm, w, late_sems.at[0])
    w_copy.start()
    loads = []
    first = 0
    for t, size in enumerate(tiles):
        at = pl.ds(first, size)
        loads.append((
            first, size,
            pltpu.make_async_copy(adj_hbm.at[:, at], adj.at[:, at], sems.at[t, 0]),
            pltpu.make_async_copy(met_hbm.at[:, at], met.at[:, at], sems.at[t, 1]),
        ))
        first += size
    for _, _, one, two in loads:
        one.start()
        two.start()
    late = [
        pltpu.make_async_copy(src_hbm.at[pl.ds(0, NODES), :], src, late_sems.at[1]),
        pltpu.make_async_copy(jac_hbm.at[0], jac, late_sems.at[2]),
        pltpu.make_async_copy(face_hbm, face, late_sems.at[3]),
    ]
    for copy in late:
        copy.start()

    rows[0:8, :] = jnp.zeros((8, LANES), F32)
    step = 256
    upper = (iota((step, step), 0) < iota((step, step), 1)).astype(BF16)
    j = iota((LANES, step), 0)
    krow = jnp.where(j < 48, j % CAP, jnp.where(j < 64, -1, jnp.where(j < 112, (j - 64) % CAP, -1)))
    carry = jnp.zeros((n_dev, 1), F32)
    table = jnp.zeros((n_dev, LANES), F32)
    table_t = jnp.zeros((LANES, n_dev), F32)
    for c in range(n_rec // step):
        at = slice(c * step, (c + 1) * step)
        live = (iota((1, step), 1) + c * step) < cnt_ref[0]
        hit = (iota((n_dev, step), 0) == owner_ref[:, at]) & live
        a = jnp.where(hit, 1.0, 0.0).astype(F32)
        ab = a.astype(BF16)
        before = dot(ab, upper, DOT10) + carry
        rank = jnp.sum(a * before, axis=0, keepdims=True).astype(jnp.int32)
        carry = carry + jnp.sum(a, axis=1, keepdims=True)
        tag = dblk_ref[:, at] + 1
        at_row = recv_ref[:, at] * 2 + slot_ref[:, at] + 2
        feature = jnp.where(j < 24, at_row >> 7, jnp.where(j < 48, at_row & 127, jnp.where(j < 88, tag >> 5, tag & 31)))
        z = jnp.where(krow == rank, feature, 0).astype(F32).astype(BF16)
        table = table + dot(ab, z, DOT11)
        table_t = table_t + dot(z, ab, DOT11)
    numbers[...] = table
    place = (table_t[0:24] * 512.0 + table_t[24:48] * 4.0).astype(jnp.int32)
    for k in range(CAP):
        place_v[0:1, k * n_dev:(k + 1) * n_dev] = place[k:k + 1]
    place_copy = pltpu.make_async_copy(place_v, place_s, sem)
    place_copy.start()

    w_copy.wait()
    wcat[:, 0:256] = w[0, :, 0:256]
    wcat[:, 256:512] = w[1, :, 0:256]
    wcat[:, 512:640] = jnp.concatenate([w[0, :, 256:320], w[1, :, 256:320]], axis=1)
    s_all = jnp.zeros((adj.shape[0], LANES), F32)
    s_face = jnp.zeros((adj.shape[0], LANES), F32)
    for first, size, one, two in loads:
        one.wait()
        two.wait()
        for start in range(first, first + size, 512):
            at = slice(start, start + 512)
            x = product(adj[:, at], met[:, at])
            y = dot(x, wcat[...], DOT00)
            base = (start + 1) * 8
            p2 = y[:, 512:640]
            for k, piece in ((0, y[:, 0:128]), (1, y[:, 128:256]), (2, p2), (4, y[:, 256:384]), (5, y[:, 384:512]), (6, pltpu.roll(p2, 64, 1))):
                rows[pl.ds(base + k, 512, stride=8), :] = piece
            xf = x.astype(F32)
            for g in range(0, 512, LANES):
                s_all = s_all + xf[:, g:g + LANES]
                if start + g < ifb:
                    s_face = s_face + xf[:, g:g + LANES]
    for copy in late:
        copy.wait()
    jsum = jnp.sum(jac[:, 0:NODES].astype(F32), axis=1, keepdims=True)
    fsum = jnp.sum(face[:, 0:NODES].astype(F32), axis=1, keepdims=True)
    own_mass = jnp.sum(s_all * jsum + s_face * fsum, keepdims=True) - jnp.sum(src[...].astype(F32), keepdims=True)

    place_copy.wait()
    group = stage.shape[1]
    groups = n_dev // group
    lane8 = iota((8, LANES), 1)

    def gather(g, buf):
        for u in range(group):
            for k in range(CAP):
                at = pl.multiple_of(place_s[0, k * n_dev + g * group + u], 4)
                stage[buf, u, k * 4:k * 4 + 4, :] = rows[pl.ds(at, 4), :]

    def emit(g, buf, acc):
        for u in range(group):
            d = g * group + u
            p0, p1, p2 = [stage[buf, u, pl.ds(i, CAP, stride=4), :] for i in range(3)]
            low = jnp.where(lane8 < 64, p2[0:8], pltpu.roll(p2[16:24], 64, 1))
            high = jnp.where(lane8 < 64, p2[8:16], jnp.broadcast_to(numbers[pl.ds(d, 1), :], (8, LANES)))
            block = jnp.concatenate([p0[0:16], p1[0:16], p0[16:24], p1[16:24], low, high], axis=0).astype(BF16)
            send_ref[d] = block
            q = block.astype(F32)
            acc = acc + (q[0:8] + q[8:16] + q[32:40])
        return acc

    gather(0, 0)

    def both(i, acc):
        gather(2 * i + 1, 1)
        acc = emit(2 * i, 0, acc)
        gather(jnp.minimum(2 * i + 2, groups - 1), 0)
        return emit(2 * i + 1, 1, acc)

    acc = lax.fori_loop(0, groups // 2, both, jnp.zeros((8, LANES), F32))
    mass = own_mass + jnp.sum(jnp.where(lane8 < NODES, acc, 0.0), keepdims=True)
    m0 = mass.astype(BF16).astype(F32)
    m1 = (mass - m0).astype(BF16).astype(F32)
    m2 = mass - m0 - m1
    lane = iota((16, LANES), 1)
    add = jnp.where(lane == 112, m0, jnp.where(lane == 113, m1, jnp.where(lane == 114, m2, 0.0)))
    add = jnp.where(iota((16, LANES), 0) >= 8, add, 0.0).astype(BF16)

    def put(d, _):
        send_ref[d, 48:64, :] += add
        return 0

    lax.fori_loop(0, n_dev, put, 0, unroll=8)


def pack(cnt, owner, recv, slot, dblk, adj, met, src, jac, face, weights, n_dev, ifb=384):
    width, blocks = adj.shape
    n_rec = owner.shape[1]
    tiles = (2048, 2048)
    hbm = pl.BlockSpec(memory_space=pl.ANY)
    vmem = pl.BlockSpec(memory_space=pltpu.VMEM)
    return pl.pallas_call(
        functools.partial(pack_kernel, tiles, ifb),
        in_specs=[pl.BlockSpec(memory_space=pltpu.SMEM)] + [vmem] * 4 + [hbm] * 6,
        out_specs=vmem,
        out_shape=jax.ShapeDtypeStruct((n_dev, 64, LANES), BF16),
        scratch_shapes=[
            pltpu.VMEM((width, blocks), BF16),
            pltpu.VMEM((width, blocks), BF16),
            pltpu.VMEM((NODES, blocks), BF16),
            pltpu.VMEM((width, width), BF16),
            pltpu.VMEM((width, width), BF16),
            pltpu.VMEM((2, width, width), BF16),
            pltpu.VMEM((width, 640), BF16),
            pltpu.VMEM(((blocks + 1) * 8, LANES), F32),
            pltpu.VMEM((2, 4, CAP * 4, LANES), F32),
            pltpu.VMEM((1, CAP * n_dev), jnp.int32),
            pltpu.SMEM((1, CAP * n_dev), jnp.int32),
            pltpu.VMEM((n_dev, LANES), F32),
            pltpu.SemaphoreType.DMA((len(tiles), 2)),
            pltpu.SemaphoreType.DMA((4,)),
            pltpu.SemaphoreType.DMA,
        ],
        compiler_params=pltpu.CompilerParams(vmem_limit_bytes=VMEM_LIMIT),
        cost_estimate=pl.CostEstimate(flops=2 * blocks * width * 2 * width, bytes_accessed=8 << 20, transcendentals=0),
        name="pack",
    )(cnt, owner, recv, slot, dblk, adj, met, src, jac, face, weights)


def face_out_kernel(adj_ref, met_ref, nbr_ref, out_ref):
    width, ifb = adj_ref.shape
    out_ref[0:width, :] = product(adj_ref[...], met_ref[...])
    nbr = nbr_ref[...]
    r = iota((16, ifb), 0)
    out_ref[width:width + 16, :] = jnp.where(r < 8, nbr >> 5, nbr & 31).astype(F32).astype(BF16)


def face_out(adj, met, nbr):
    width, _ = adj.shape
    ifb = nbr.shape[1]
    return pl.pallas_call(
        face_out_kernel,
        grid=(1,),
        in_specs=[
            pl.BlockSpec((width, ifb), lambda t: (0, 0)),
            pl.BlockSpec((width, ifb), lambda t: (0, 0)),
            pl.BlockSpec((1, ifb), lambda t: (0, 0)),
        ],
        out_specs=pl.BlockSpec((width + 16, ifb), lambda t: (0, 0)),
        out_shape=jax.ShapeDtypeStruct((width + 16, ifb), BF16),
        compiler_params=pltpu.CompilerParams(vmem_limit_bytes=VMEM_LIMIT),
        name="face_out",
    )(adj, met, nbr)


def partial_kernel(me_ref, adj_ref, met_ref, src_ref, jac_ref, face_ref, *rest):
    got_refs, out_ref = rest[:-1], rest[-1]
    t = pl.program_id(0)
    width = adj_ref.shape[0]
    x = product(adj_ref[...], met_ref[...])
    out_ref[...] = dot(jac_ref[0], x, DOT00) - src_ref[...].astype(F32)

    @pl.when(t == 0)
    def _():
        ifb = got_refs[0].shape[1]
        acc = jnp.zeros((width, ifb), F32)
        for got_ref in got_refs:
            term = dot(face_ref[...], got_ref[0:width, :], DOT00)
            number = got_ref[width:width + 16, :].astype(F32)
            nbr = (number[0:1] * 32.0 + number[8:9]).astype(jnp.int32) - me_ref[0] * ifb
            hit = jnp.where(iota((ifb, ifb), 0) == nbr, 1.0, 0.0).astype(F32).astype(BF16)
            acc = acc + dot(term.astype(BF16), hit, DOT11)
        out_ref[:, 0:ifb] += acc


def partial_total(me, adj, met, src, jac, face, faces):
    width, blocks = adj.shape
    tile = 512
    col = lambda t: (0, t)
    return pl.pallas_call(
        partial_kernel,
        grid=(blocks // tile,),
        in_specs=[
            pl.BlockSpec(memory_space=pltpu.SMEM),
            pl.BlockSpec((width, tile), col),
            pl.BlockSpec((width, tile), col),
            pl.BlockSpec((width, tile), col),
            pl.BlockSpec((1, width, width), lambda t: (0, 0, 0)),
            pl.BlockSpec((width, width), lambda t: (0, 0)),
        ] + [pl.BlockSpec(faces[0].shape, lambda t: (0, 0))] * len(faces),
        out_specs=pl.BlockSpec((width, tile), col),
        out_shape=jax.ShapeDtypeStruct((width, blocks), F32),
        compiler_params=pltpu.CompilerParams(vmem_limit_bytes=VMEM_LIMIT),
        cost_estimate=pl.CostEstimate(flops=2 * blocks * width * width, bytes_accessed=13 << 20, transcendentals=0),
        name="partial",
    )(me, adj, met, src, jac, face, *faces)


def unpack_kernel(scale, got_hbm, part_hbm, out_hbm, mass_ref, got, part, out, q_t, index, q, numbers, hit, got_sems, part_sems, out_sems):
    n_dev = got.shape[0]
    slots = n_dev * CAP
    width, blocks = out.shape
    tile = hit.shape[2]
    n_tiles = blocks // tile
    n_got, n_part = got_sems.shape[0], part_sems.shape[0]
    g_size, p_size = n_dev // n_got, blocks // n_part
    got_in = [pltpu.make_async_copy(got_hbm.at[pl.ds(i * g_size, g_size)], got.at[pl.ds(i * g_size, g_size)], got_sems.at[i]) for i in range(n_got)]
    part_in = [pltpu.make_async_copy(part_hbm.at[:, pl.ds(i * p_size, p_size)], part.at[:, pl.ds(i * p_size, p_size)], part_sems.at[i]) for i in range(n_part)]
    for copy in got_in + part_in:
        copy.start()

    def take(s, _):
        g = got[s].astype(F32)
        at = pl.multiple_of(s * CAP, 8)
        q[pl.ds(at, 16), 0:128] = g[0:16]
        q[pl.ds(at, 16), 128:256] = g[16:32]
        q[pl.ds(at + 16, 8), 0:128] = g[32:40]
        q[pl.ds(at + 16, 8), 128:256] = g[40:48]
        q[pl.ds(at, 16), 256:384] = g[48:64]
        q[pl.ds(at + 16, 8), 256:384] = pltpu.roll(g[48:56], 64, 1)
        numbers[pl.ds(s, 1), :] = g[56:57]
        return 0

    for i in range(n_got):
        got_in[i].wait()
        lax.fori_loop(i * g_size, (i + 1) * g_size, take, 0, unroll=8)

    nums = numbers[...]
    lane = iota((n_dev, LANES), 1)
    mass_ref[0, 0] = jnp.sum(jnp.where((lane >= 112) & (lane < 115), nums, 0.0)) * scale
    nums = nums.astype(BF16)
    rows = 16 * CAP
    row = iota((rows, LANES), 0)
    lane = iota((rows, LANES), 1)
    k = row % CAP
    pick = jnp.where(lane - 64 == k, 32.0, jnp.where(lane - 88 == k, 1.0, 0.0)).astype(F32)
    for c in range(n_dev // 16):
        source = jnp.where(lane == row // CAP + 16 * c, 1.0, 0.0).astype(F32).astype(BF16)
        value = jnp.sum(dot(source, nums, DOT10) * pick, axis=1, keepdims=True)
        index[c * rows:(c + 1) * rows, :] = jnp.broadcast_to(value.astype(jnp.int32) - 1, (rows, LANES))
    step = 256
    for c in range(slots // step):
        at = slice(c * step, (c + 1) * step)
        q_t[:, at] = q[at, :].T[0:width].astype(BF16)

    lane = iota((step, LANES), 1)

    def mark(n, buf):
        for c in range(slots // step):
            at = slice(c * step, (c + 1) * step)
            ids = index[at, :] - n * tile
            for g in range(0, tile, LANES):
                hit[buf, at, g:g + LANES] = jnp.where(ids == lane + g, 1.0, 0.0).astype(F32).astype(BF16)

    def out_copy(n):
        at = pl.ds(pl.multiple_of(n * tile, tile), tile)
        return pltpu.make_async_copy(out.at[:, at], out_hbm.at[:, at], out_sems.at[n])

    def add(n, buf):
        at = pl.ds(pl.multiple_of(n * tile, tile), tile)
        out[:, at] = (part[:, at] + dot(q_t[...], hit[buf], DOT10)).astype(BF16)
        out_copy(n).start()

    mark(0, 0)
    for copy in part_in:
        copy.wait()

    def both(i, _):
        mark(2 * i + 1, 1)
        add(2 * i, 0)
        mark(2 * i + 2, 0)
        add(2 * i + 1, 1)
        return 0

    lax.fori_loop(0, n_tiles // 2, both, 0)

    def finish(n, _):
        out_copy(n).wait()
        return 0

    lax.fori_loop(0, n_tiles, finish, 0)


def unpack(got, part, scale):
    width, blocks = part.shape
    n_dev = got.shape[0]
    tile = 512
    slots = n_dev * CAP
    hbm = pl.BlockSpec(memory_space=pl.ANY)
    return pl.pallas_call(
        functools.partial(unpack_kernel, scale),
        in_specs=[hbm, hbm],
        out_specs=[hbm, pl.BlockSpec(memory_space=pltpu.SMEM)],
        out_shape=[
            jax.ShapeDtypeStruct((width, blocks), BF16),
            jax.ShapeDtypeStruct((1, 1), F32),
        ],
        scratch_shapes=[
            pltpu.VMEM(got.shape, BF16),
            pltpu.VMEM((width, blocks), F32),
            pltpu.VMEM((width, blocks), BF16),
            pltpu.VMEM((width, slots), BF16),
            pltpu.VMEM((slots, LANES), jnp.int32),
            pltpu.VMEM((slots, 384), F32),
            pltpu.VMEM((n_dev, LANES), F32),
            pltpu.VMEM((2, slots, tile), BF16),
            pltpu.SemaphoreType.DMA((4,)),
            pltpu.SemaphoreType.DMA((4,)),
            pltpu.SemaphoreType.DMA((blocks // tile,)),
        ],
        compiler_params=pltpu.CompilerParams(vmem_limit_bytes=VMEM_LIMIT),
        cost_estimate=pl.CostEstimate(flops=2 * blocks * slots * width, bytes_accessed=10 << 20, transcendentals=0),
        name="unpack",
    )(got, part)


def shards(
    adjoint, metric, comp_jac, face_jac, donor_weights, source, face_nbr,
    receiver_block, donor_owner, donor_block, donor_slot, fringe_count,
):
    blocks, width = adjoint.shape
    n_dev = lax.axis_size("comp") * lax.axis_size("blk")
    adj, met, src = adjoint.T, metric.T, source.T
    row = lambda a: a.reshape(1, -1)
    own = face_out(adj, met, row(face_nbr))
    n_comp = lax.axis_size("comp")
    faces = [own] + [
        lax.ppermute(own, "comp", [(i, (i + k) % n_comp) for i in range(n_comp)]) for k in range(1, n_comp)
    ]
    send = pack(
        fringe_count, row(donor_owner), row(receiver_block), row(donor_slot), row(donor_block),
        adj, met, src, comp_jac, face_jac, donor_weights, n_dev,
    )
    got = lax.all_to_all(send, ("comp", "blk"), split_axis=0, concat_axis=0, tiled=True)
    me = lax.axis_index("comp").astype(jnp.int32).reshape(1)
    part = partial_total(me, adj, met, src, comp_jac, face_jac, faces)
    out, mass = unpack(got, part, 1.0 / float(blocks * n_dev * NODES) ** 0.5)
    return out.T, mass.reshape(())


def solution(mesh):
    both = ("comp", "blk")
    placed = (
        P(both, None), P(both, None), P("comp", None, None), P(), P(), P(both, None),
        P(both), P(both), P(both, None), P(both), P(both), P(both),
    )
    return jax.shard_map(
        shards, mesh=mesh, in_specs=placed, out_specs=(P(both, None), P()), check_vma=False,
    )
```

```python
import functools

import jax
import jax.numpy as jnp
from jax import lax
from jax.experimental import pallas as pl
from jax.experimental.pallas import tpu as pltpu
from jax.sharding import PartitionSpec as P

NODES = 64
CAP = 24
LANES = 128
DOT00 = (((0,), (0,)), ((), ()))
DOT11 = (((1,), (1,)), ((), ()))
DOT10 = (((1,), (0,)), ((), ()))
F32 = jnp.float32
BF16 = jnp.bfloat16
VMEM_LIMIT = 60 * 1024 * 1024


def dot(a, b, dims):
    return lax.dot_general(a, b, dims, preferred_element_type=F32)


def iota(shape, axis):
    return lax.broadcasted_iota(jnp.int32, shape, axis)


def product(a, b):
    return (a.astype(F32) * b.astype(F32)).astype(BF16)


def pack_kernel(
    tiles, ifb, cnt_ref, owner_ref, recv_ref, slot_ref, dblk_ref, adj_hbm, met_hbm, src_hbm, jac_hbm, face_hbm, w_hbm,
    send_ref, adj, met, src, jac, face, w, wcat, rows, stage, place_v, place_s, numbers, sems, late_sems, sem,
):
    n_dev = send_ref.shape[0]
    n_rec = owner_ref.shape[1]

    w_copy = pltpu.make_async_copy(w_hbm, w, late_sems.at[0])
    w_copy.start()
    loads = []
    first = 0
    for t, size in enumerate(tiles):
        at = pl.ds(first, size)
        loads.append((
            first, size,
            pltpu.make_async_copy(adj_hbm.at[:, at], adj.at[:, at], sems.at[t, 0]),
            pltpu.make_async_copy(met_hbm.at[:, at], met.at[:, at], sems.at[t, 1]),
        ))
        first += size
    for _, _, one, two in loads:
        one.start()
        two.start()
    late = [
        pltpu.make_async_copy(src_hbm.at[pl.ds(0, NODES), :], src, late_sems.at[1]),
        pltpu.make_async_copy(jac_hbm.at[0], jac, late_sems.at[2]),
        pltpu.make_async_copy(face_hbm, face, late_sems.at[3]),
    ]
    for copy in late:
        copy.start()

    rows[0:8, :] = jnp.zeros((8, LANES), F32)
    step = 256
    upper = (iota((step, step), 0) < iota((step, step), 1)).astype(BF16)
    j = iota((LANES, step), 0)
    krow = jnp.where(j < 48, j % CAP, jnp.where(j < 64, -1, jnp.where(j < 112, (j - 64) % CAP, -1)))
    carry = jnp.zeros((n_dev, 1), F32)
    table = jnp.zeros((n_dev, LANES), F32)
    table_t = jnp.zeros((LANES, n_dev), F32)
    for c in range(n_rec // step):
        at = slice(c * step, (c + 1) * step)
        live = (iota((1, step), 1) + c * step) < cnt_ref[0]
        hit = (iota((n_dev, step), 0) == owner_ref[:, at]) & live
        a = jnp.where(hit, 1.0, 0.0).astype(F32)
        ab = a.astype(BF16)
        before = dot(ab, upper, DOT10) + carry
        rank = jnp.sum(a * before, axis=0, keepdims=True).astype(jnp.int32)
        carry = carry + jnp.sum(a, axis=1, keepdims=True)
        tag = dblk_ref[:, at] + 1
        at_row = recv_ref[:, at] * 2 + slot_ref[:, at] + 2
        feature = jnp.where(j < 24, at_row >> 7, jnp.where(j < 48, at_row & 127, jnp.where(j < 88, tag >> 5, tag & 31)))
        z = jnp.where(krow == rank, feature, 0).astype(F32).astype(BF16)
        table = table + dot(ab, z, DOT11)
        table_t = table_t + dot(z, ab, DOT11)
    numbers[...] = table
    place = (table_t[0:24] * 512.0 + table_t[24:48] * 4.0).astype(jnp.int32)
    for k in range(CAP):
        place_v[0:1, k * n_dev:(k + 1) * n_dev] = place[k:k + 1]
    place_copy = pltpu.make_async_copy(place_v, place_s, sem)
    place_copy.start()

    w_copy.wait()
    wcat[:, 0:256] = w[0, :, 0:256]
    wcat[:, 256:512] = w[1, :, 0:256]
    wcat[:, 512:640] = jnp.concatenate([w[0, :, 256:320], w[1, :, 256:320]], axis=1)
    s_all = jnp.zeros((adj.shape[0], LANES), F32)
    s_face = jnp.zeros((adj.shape[0], LANES), F32)
    for first, size, one, two in loads:
        one.wait()
        two.wait()
        for start in range(first, first + size, 512):
            at = slice(start, start + 512)
            x = product(adj[:, at], met[:, at])
            y = dot(x, wcat[...], DOT00)
            base = (start + 1) * 8
            p2 = y[:, 512:640]
            for k, piece in ((0, y[:, 0:128]), (1, y[:, 128:256]), (2, p2), (4, y[:, 256:384]), (5, y[:, 384:512]), (6, pltpu.roll(p2, 64, 1))):
                rows[pl.ds(base + k, 512, stride=8), :] = piece
            xf = x.astype(F32)
            for g in range(0, 512, LANES):
                s_all = s_all + xf[:, g:g + LANES]
                if start + g < ifb:
                    s_face = s_face + xf[:, g:g + LANES]
    for copy in late:
        copy.wait()
    jsum = jnp.sum(jac[:, 0:NODES].astype(F32), axis=1, keepdims=True)
    fsum = jnp.sum(face[:, 0:NODES].astype(F32), axis=1, keepdims=True)
    own_mass = jnp.sum(s_all * jsum + s_face * fsum, keepdims=True) - jnp.sum(src[...].astype(F32), keepdims=True)

    place_copy.wait()
    group = stage.shape[1]
    groups = n_dev // group
    lane8 = iota((8, LANES), 1)

    def gather(g, buf):
        for u in range(group):
            for k in range(CAP):
                at = pl.multiple_of(place_s[0, k * n_dev + g * group + u], 4)
                stage[buf, u, k * 4:k * 4 + 4, :] = rows[pl.ds(at, 4), :]

    def emit(g, buf, acc):
        for u in range(group):
            d = g * group + u
            p0, p1, p2 = [stage[buf, u, pl.ds(i, CAP, stride=4), :] for i in range(3)]
            low = jnp.where(lane8 < 64, p2[0:8], pltpu.roll(p2[16:24], 64, 1))
            high = jnp.where(lane8 < 64, p2[8:16], jnp.broadcast_to(numbers[pl.ds(d, 1), :], (8, LANES)))
            block = jnp.concatenate([p0[0:16], p1[0:16], p0[16:24], p1[16:24], low, high], axis=0).astype(BF16)
            send_ref[d] = block
            q = block.astype(F32)
            acc = acc + (q[0:8] + q[8:16] + q[32:40])
        return acc

    gather(0, 0)

    def both(i, acc):
        gather(2 * i + 1, 1)
        acc = emit(2 * i, 0, acc)
        gather(jnp.minimum(2 * i + 2, groups - 1), 0)
        return emit(2 * i + 1, 1, acc)

    acc = lax.fori_loop(0, groups // 2, both, jnp.zeros((8, LANES), F32))
    mass = own_mass + jnp.sum(jnp.where(lane8 < NODES, acc, 0.0), keepdims=True)
    m0 = mass.astype(BF16).astype(F32)
    m1 = (mass - m0).astype(BF16).astype(F32)
    m2 = mass - m0 - m1
    lane = iota((16, LANES), 1)
    add = jnp.where(lane == 112, m0, jnp.where(lane == 113, m1, jnp.where(lane == 114, m2, 0.0)))
    add = jnp.where(iota((16, LANES), 0) >= 8, add, 0.0).astype(BF16)

    def put(d, _):
        send_ref[d, 48:64, :] += add
        return 0

    lax.fori_loop(0, n_dev, put, 0, unroll=8)


def pack(cnt, owner, recv, slot, dblk, adj, met, src, jac, face, weights, n_dev, ifb=384):
    width, blocks = adj.shape
    n_rec = owner.shape[1]
    tiles = (2048, 2048)
    hbm = pl.BlockSpec(memory_space=pl.ANY)
    vmem = pl.BlockSpec(memory_space=pltpu.VMEM)
    return pl.pallas_call(
        functools.partial(pack_kernel, tiles, ifb),
        in_specs=[pl.BlockSpec(memory_space=pltpu.SMEM)] + [vmem] * 4 + [hbm] * 6,
        out_specs=vmem,
        out_shape=jax.ShapeDtypeStruct((n_dev, 64, LANES), BF16),
        scratch_shapes=[
            pltpu.VMEM((width, blocks), BF16),
            pltpu.VMEM((width, blocks), BF16),
            pltpu.VMEM((NODES, blocks), BF16),
            pltpu.VMEM((width, width), BF16),
            pltpu.VMEM((width, width), BF16),
            pltpu.VMEM((2, width, width), BF16),
            pltpu.VMEM((width, 640), BF16),
            pltpu.VMEM(((blocks + 1) * 8, LANES), F32),
            pltpu.VMEM((2, 4, CAP * 4, LANES), F32),
            pltpu.VMEM((1, CAP * n_dev), jnp.int32),
            pltpu.SMEM((1, CAP * n_dev), jnp.int32),
            pltpu.VMEM((n_dev, LANES), F32),
            pltpu.SemaphoreType.DMA((len(tiles), 2)),
            pltpu.SemaphoreType.DMA((4,)),
            pltpu.SemaphoreType.DMA,
        ],
        compiler_params=pltpu.CompilerParams(vmem_limit_bytes=VMEM_LIMIT),
        cost_estimate=pl.CostEstimate(flops=2 * blocks * width * 2 * width, bytes_accessed=8 << 20, transcendentals=0),
        name="pack",
    )(cnt, owner, recv, slot, dblk, adj, met, src, jac, face, weights)


def face_out_kernel(adj_ref, met_ref, nbr_ref, out_ref):
    width, ifb = adj_ref.shape
    out_ref[0:width, :] = product(adj_ref[...], met_ref[...])
    nbr = nbr_ref[...].reshape(1, ifb)
    r = iota((16, ifb), 0)
    out_ref[width:width + 16, :] = jnp.where(r < 8, nbr >> 5, nbr & 31).astype(F32).astype(BF16)


def face_out(adj, met, nbr):
    width, _ = adj.shape
    ifb = nbr.shape[0]
    return pl.pallas_call(
        face_out_kernel,
        grid=(1,),
        in_specs=[
            pl.BlockSpec((width, ifb), lambda t: (0, 0)),
            pl.BlockSpec((width, ifb), lambda t: (0, 0)),
            pl.BlockSpec((ifb,), lambda t: (0,)),
        ],
        out_specs=pl.BlockSpec((width + 16, ifb), lambda t: (0, 0)),
        out_shape=jax.ShapeDtypeStruct((width + 16, ifb), BF16),
        compiler_params=pltpu.CompilerParams(vmem_limit_bytes=VMEM_LIMIT),
        name="face_out",
    )(adj, met, nbr)


def partial_kernel(me_ref, adj_ref, met_ref, src_ref, jac_ref, face_ref, *rest):
    got_refs, out_ref = rest[:-1], rest[-1]
    t = pl.program_id(0)
    width = adj_ref.shape[0]
    x = product(adj_ref[...], met_ref[...])
    out_ref[...] = dot(jac_ref[0], x, DOT00) - src_ref[...].astype(F32)

    @pl.when(t == 0)
    def _():
        ifb = got_refs[0].shape[1]
        acc = jnp.zeros((width, ifb), F32)
        for got_ref in got_refs:
            term = dot(face_ref[...], got_ref[0:width, :], DOT00)
            number = got_ref[width:width + 16, :].astype(F32)
            nbr = (number[0:1] * 32.0 + number[8:9]).astype(jnp.int32) - me_ref[0] * ifb
            hit = jnp.where(iota((ifb, ifb), 0) == nbr, 1.0, 0.0).astype(F32).astype(BF16)
            acc = acc + dot(term.astype(BF16), hit, DOT11)
        out_ref[:, 0:ifb] += acc


def partial_total(me, adj, met, src, jac, face, faces):
    width, blocks = adj.shape
    tile = 512
    col = lambda t: (0, t)
    return pl.pallas_call(
        partial_kernel,
        grid=(blocks // tile,),
        in_specs=[
            pl.BlockSpec(memory_space=pltpu.SMEM),
            pl.BlockSpec((width, tile), col),
            pl.BlockSpec((width, tile), col),
            pl.BlockSpec((width, tile), col),
            pl.BlockSpec((1, width, width), lambda t: (0, 0, 0)),
            pl.BlockSpec((width, width), lambda t: (0, 0)),
        ] + [pl.BlockSpec(faces[0].shape, lambda t: (0, 0))] * len(faces),
        out_specs=pl.BlockSpec((width, tile), col),
        out_shape=jax.ShapeDtypeStruct((width, blocks), F32),
        compiler_params=pltpu.CompilerParams(vmem_limit_bytes=VMEM_LIMIT),
        cost_estimate=pl.CostEstimate(flops=2 * blocks * width * width, bytes_accessed=13 << 20, transcendentals=0),
        name="partial",
    )(me, adj, met, src, jac, face, *faces)


ROOM = 192
BUCKET = 256


def unpack_kernel(
    scale, got_hbm, part_hbm, out_hbm, mass_ref,
    got, part, out, q, stage, numbers, bucket, rank, low, place_v, place_s, ids, in_sems, out_sems, sem,
):
    n_dev = got.shape[0]
    width, blocks = out.shape
    n_buckets = blocks // BUCKET
    got_in = pltpu.make_async_copy(got_hbm, got, in_sems.at[0])
    part_in = pltpu.make_async_copy(part_hbm, part, in_sems.at[1])
    got_in.start()
    q[0:8, :] = jnp.zeros((8, LANES), F32)
    got_in.wait()
    part_in.start()

    def number(s, _):
        numbers[pl.ds(s, 1), :] = got[s, 48:64, :].astype(F32)[8:9]
        return 0

    lax.fori_loop(0, n_dev, number, 0, unroll=16)

    lane = iota((n_dev, LANES), 1)
    nums = numbers[...]
    mass_ref[0, 0] = jnp.sum(jnp.where((lane >= 112) & (lane < 115), nums, 0.0)) * scale
    nums = nums.T
    block = (nums[64:64 + CAP] * 32.0 + nums[64 + CAP:64 + 2 * CAP]).astype(jnp.int32) - 1
    bucket[...] = block >> 8
    low[...] = (block & 255) + 1

    def hits(k):
        return jnp.where(iota((n_buckets, LANES), 0) == bucket[k:k + 1, :], 1.0, 0.0).astype(F32)

    upper = (iota((LANES, LANES), 0) < iota((LANES, LANES), 1)).astype(BF16)
    hit = [hits(k) for k in range(CAP)]
    before = dot(jnp.concatenate(hit, axis=0).astype(BF16), upper, DOT10)
    carry = jnp.zeros((n_buckets, 1), F32)
    for k in range(CAP):
        at = k * n_buckets
        rank[k:k + 1, :] = jnp.sum(hit[k] * (before[at:at + n_buckets] + carry), axis=0, keepdims=True).astype(jnp.int32)
        carry = carry + jnp.sum(hit[k], axis=1, keepdims=True)
    rounds = (jnp.max(carry).astype(jnp.int32) + ROOM - 1) // ROOM

    def choose(turn):
        table = jnp.zeros((n_buckets, 2 * ROOM), F32)
        inside = jnp.zeros((ROOM, n_buckets), F32)
        wide = lambda ref, k: jnp.concatenate([ref[k:k + 1, :], ref[k + 1:k + 2, :]], axis=1)
        for k in range(0, CAP, 2):
            here = iota((ROOM, 2 * LANES), 0) == wide(rank, k) - turn * ROOM
            l = iota((1, 2 * LANES), 1)
            record = (l & (LANES - 1)) * CAP + (l >> 7) + k + 2
            pair = jnp.concatenate([hits(k), hits(k + 1)], axis=1).astype(BF16)
            mark = lambda v: jnp.where(here, v, 0).astype(F32).astype(BF16)
            table = table + dot(pair, jnp.concatenate([mark(record >> 6), mark(record & 63)], axis=0), DOT11)
            inside = inside + dot(mark(wide(low, k)), pair, DOT11)
        place_v[:, 0:ROOM] = (table[:, 0:ROOM] * 256.0 + table[:, ROOM:] * 4.0).astype(jnp.int32)
        ids[:, 0:n_buckets] = inside.astype(jnp.int32) - 1
        return pltpu.make_async_copy(place_v, place_s, sem)

    def gather(b, buf):
        for p in range(ROOM):
            at = pl.multiple_of(place_s[b, p], 4)
            stage[buf, p * 4:p * 4 + 4, :] = q[pl.ds(at, 4), :]

    def added(b, buf):
        rows = jnp.concatenate([stage[buf, pl.ds(i, ROOM, stride=4), :].astype(BF16) for i in range(3)], axis=1)
        mine = jnp.sum(jnp.where(iota((ROOM, n_buckets), 1) == b, ids[:, 0:n_buckets], 0), axis=1, keepdims=True)
        mark = jnp.where(iota((ROOM, BUCKET), 1) == mine, 1.0, 0.0).astype(F32).astype(BF16)
        at = pl.ds(pl.multiple_of(b * BUCKET, BUCKET), BUCKET)
        return part[:, at] + dot(rows, mark, DOT00)[0:width]

    def take(s, _):
        g = got[s].astype(F32)
        at = (s * CAP + 2) * 4
        q[pl.ds(at, 16, stride=4), :] = g[0:16]
        q[pl.ds(at + 1, 16, stride=4), :] = g[16:32]
        q[pl.ds(at + 2, 16, stride=4), :] = g[48:64]
        q[pl.ds(at + 64, 8, stride=4), :] = g[32:40]
        q[pl.ds(at + 65, 8, stride=4), :] = g[40:48]
        q[pl.ds(at + 66, 8, stride=4), :] = pltpu.roll(g[48:56], 64, 1)
        return 0

    place_copy = choose(0)
    place_copy.start()
    lax.fori_loop(0, n_dev, take, 0, unroll=8)
    part_in.wait()
    place_copy.wait()

    def more(turn, _):
        copy = choose(turn)
        copy.start()
        copy.wait()

        def one(b, _):
            gather(b, 0)
            at = pl.ds(pl.multiple_of(b * BUCKET, BUCKET), BUCKET)
            part[:, at] = added(b, 0)
            return 0

        return lax.fori_loop(0, n_buckets, one, 0)

    @pl.when(rounds > 1)
    def _():
        lax.fori_loop(1, rounds, more, 0)
        again = choose(0)
        again.start()
        again.wait()

    def out_copy(i):
        at = pl.ds(pl.multiple_of(i * 2 * BUCKET, 2 * BUCKET), 2 * BUCKET)
        return pltpu.make_async_copy(out.at[:, at], out_hbm.at[:, at], out_sems.at[i])

    def put(b, buf):
        at = pl.ds(pl.multiple_of(b * BUCKET, BUCKET), BUCKET)
        out[:, at] = added(b, buf).astype(BF16)

    gather(0, 0)

    def both(i, _):
        gather(2 * i + 1, 1)
        put(2 * i, 0)
        gather(jnp.minimum(2 * i + 2, n_buckets - 1), 0)
        put(2 * i + 1, 1)
        out_copy(i).start()
        return 0

    lax.fori_loop(0, n_buckets // 2, both, 0)

    def finish(i, _):
        out_copy(i).wait()
        return 0

    lax.fori_loop(0, n_buckets // 2, finish, 0)


def unpack(got, part, scale):
    width, blocks = part.shape
    n_dev = got.shape[0]
    n_buckets = blocks // BUCKET
    hbm = pl.BlockSpec(memory_space=pl.ANY)
    return pl.pallas_call(
        functools.partial(unpack_kernel, scale),
        in_specs=[hbm, hbm],
        out_specs=[hbm, pl.BlockSpec(memory_space=pltpu.SMEM)],
        out_shape=[
            jax.ShapeDtypeStruct((width, blocks), BF16),
            jax.ShapeDtypeStruct((1, 1), F32),
        ],
        scratch_shapes=[
            pltpu.VMEM(got.shape, BF16),
            pltpu.VMEM((width, blocks), F32),
            pltpu.VMEM((width, blocks), BF16),
            pltpu.VMEM(((n_dev * CAP + 2) * 4, LANES), F32),
            pltpu.VMEM((2, ROOM * 4, LANES), F32),
            pltpu.VMEM((n_dev, LANES), F32),
            pltpu.VMEM((CAP, n_dev), jnp.int32),
            pltpu.VMEM((CAP, n_dev), jnp.int32),
            pltpu.VMEM((CAP, n_dev), jnp.int32),
            pltpu.VMEM((n_buckets, 256), jnp.int32),
            pltpu.SMEM((n_buckets, 256), jnp.int32),
            pltpu.VMEM((ROOM, LANES), jnp.int32),
            pltpu.SemaphoreType.DMA((2,)),
            pltpu.SemaphoreType.DMA((n_buckets // 2,)),
            pltpu.SemaphoreType.DMA,
        ],
        compiler_params=pltpu.CompilerParams(vmem_limit_bytes=VMEM_LIMIT),
        cost_estimate=pl.CostEstimate(flops=2 * blocks * width * BUCKET, bytes_accessed=10 << 20, transcendentals=0),
        name="unpack",
    )(got, part)


def shards(
    adjoint, metric, comp_jac, face_jac, donor_weights, source, face_nbr,
    receiver_block, donor_owner, donor_block, donor_slot, fringe_count,
):
    blocks, width = adjoint.shape
    n_dev = lax.axis_size("comp") * lax.axis_size("blk")
    adj, met, src = adjoint.T, metric.T, source.T
    row = lambda a: a.reshape(1, -1)
    own = face_out(adj, met, face_nbr)
    n_comp = lax.axis_size("comp")
    faces = [own] + [
        lax.ppermute(own, "comp", [(i, (i + k) % n_comp) for i in range(n_comp)]) for k in range(1, n_comp)
    ]
    send = pack(
        fringe_count, row(donor_owner), row(receiver_block), row(donor_slot), row(donor_block),
        adj, met, src, comp_jac, face_jac, donor_weights, n_dev,
    )
    send, *faces = lax.optimization_barrier((send, *faces))
    got = lax.all_to_all(send, ("comp", "blk"), split_axis=0, concat_axis=0, tiled=True)
    me = lax.axis_index("comp").astype(jnp.int32).reshape(1)
    part = partial_total(me, adj, met, src, comp_jac, face_jac, faces)
    out, mass = unpack(got, part, 1.0 / float(blocks * n_dev * NODES) ** 0.5)
    return out.T, mass.reshape(())


def solution(mesh):
    both = ("comp", "blk")
    placed = (
        P(both, None), P(both, None), P("comp", None, None), P(), P(), P(both, None),
        P(both), P(both), P(both, None), P(both), P(both), P(both),
    )
    return jax.shard_map(
        shards, mesh=mesh, in_specs=placed, out_specs=(P(both, None), P()), check_vma=False,
    )
```

```python
import functools

import jax
import jax.numpy as jnp
from jax import lax
from jax.experimental import pallas as pl
from jax.experimental.pallas import tpu as pltpu
from jax.sharding import PartitionSpec as P

NODES = 64
CAP = 24
LANES = 128
DOT00 = (((0,), (0,)), ((), ()))
DOT11 = (((1,), (1,)), ((), ()))
DOT10 = (((1,), (0,)), ((), ()))
F32 = jnp.float32
BF16 = jnp.bfloat16
VMEM_LIMIT = 60 * 1024 * 1024


def dot(a, b, dims):
    return lax.dot_general(a, b, dims, preferred_element_type=F32)


def iota(shape, axis):
    return lax.broadcasted_iota(jnp.int32, shape, axis)


def product(a, b):
    return (a.astype(F32) * b.astype(F32)).astype(BF16)


def pack_kernel(
    tiles, ifb, cnt_ref, owner_ref, recv_ref, slot_ref, dblk_ref, adj_hbm, met_hbm, src_hbm, jac_hbm, face_hbm, w_hbm,
    send_hbm, send, adj, met, src, jac, face, w, wcat, rows, stage, place_v, place_s, numbers, sems, late_sems, out_sems, sem,
):
    n_dev = send.shape[0]
    n_rec = owner_ref.shape[1]

    w_copy = pltpu.make_async_copy(w_hbm, w, late_sems.at[0])
    w_copy.start()
    loads = []
    first = 0
    for t, size in enumerate(tiles):
        at = pl.ds(first, size)
        loads.append((
            first, size,
            pltpu.make_async_copy(adj_hbm.at[:, at], adj.at[:, at], sems.at[t, 0]),
            pltpu.make_async_copy(met_hbm.at[:, at], met.at[:, at], sems.at[t, 1]),
        ))
        first += size
    late = [
        pltpu.make_async_copy(src_hbm.at[pl.ds(0, NODES), :], src, late_sems.at[1]),
        pltpu.make_async_copy(jac_hbm.at[0], jac, late_sems.at[2]),
        pltpu.make_async_copy(face_hbm, face, late_sems.at[3]),
    ]
    for t, (_, _, one, two) in enumerate(loads):
        one.start()
        two.start()
        if t == 0:
            for copy in late:
                copy.start()

    rows[0:8, :] = jnp.zeros((8, LANES), F32)
    cnt = cnt_ref[...].reshape(1, 1)
    step = 256
    upper = (iota((step, step), 0) < iota((step, step), 1)).astype(BF16)
    j = iota((LANES, step), 0)
    krow = jnp.where(j < 48, j % CAP, jnp.where(j < 64, -1, jnp.where(j < 112, (j - 64) % CAP, -1)))
    carry = jnp.zeros((n_dev, 1), F32)
    table = jnp.zeros((n_dev, LANES), F32)
    table_t = jnp.zeros((LANES, n_dev), F32)
    for c in range(n_rec // step):
        at = slice(c * step, (c + 1) * step)
        live = (iota((1, step), 1) + c * step) < cnt
        hit = (iota((n_dev, step), 0) == owner_ref[:, at]) & live
        a = jnp.where(hit, 1.0, 0.0).astype(F32)
        ab = a.astype(BF16)
        before = dot(ab, upper, DOT10) + carry
        rank = jnp.sum(a * before, axis=0, keepdims=True).astype(jnp.int32)
        carry = carry + jnp.sum(a, axis=1, keepdims=True)
        tag = dblk_ref[:, at] + 1
        at_row = recv_ref[:, at] * 2 + slot_ref[:, at] + 2
        feature = jnp.where(j < 24, at_row >> 7, jnp.where(j < 48, at_row & 127, jnp.where(j < 88, tag >> 5, tag & 31)))
        z = jnp.where(krow == rank, feature, 0).astype(F32).astype(BF16)
        table = table + dot(ab, z, DOT11)
        table_t = table_t + dot(z, ab, DOT11)
    numbers[...] = table
    place = (table_t[0:24] * 512.0 + table_t[24:48] * 4.0).astype(jnp.int32)
    for k in range(CAP):
        place_v[0:1, k * n_dev:(k + 1) * n_dev] = place[k:k + 1]
    place_copy = pltpu.make_async_copy(place_v, place_s, sem)
    place_copy.start()

    w_copy.wait()
    wcat[:, 0:256] = w[0, :, 0:256]
    wcat[:, 256:512] = w[1, :, 0:256]
    wcat[:, 512:640] = jnp.concatenate([w[0, :, 256:320], w[1, :, 256:320]], axis=1)
    s_all = jnp.zeros((adj.shape[0], LANES), F32)
    s_face = jnp.zeros((adj.shape[0], LANES), F32)
    fold = lambda v: jnp.sum(v.reshape(-1, 8, LANES), axis=0)
    for first, size, one, two in loads:
        one.wait()
        two.wait()
        if first == 0:
            for copy in late:
                copy.wait()
            jsum = jnp.sum(jac[:, 0:NODES].astype(F32), axis=1, keepdims=True)
            fsum = jnp.sum(face[:, 0:NODES].astype(F32), axis=1, keepdims=True)
            src_sum = jnp.zeros((8, LANES), F32)
            for g in range(0, src.shape[1], LANES):
                src_sum = src_sum + fold(src[:, g:g + LANES].astype(F32))
        for start in range(first, first + size, 512):
            at = slice(start, start + 512)
            x = product(adj[:, at], met[:, at])
            y = dot(x, wcat[...], DOT00)
            base = (start + 1) * 8
            p2 = y[:, 512:640]
            for k, piece in ((0, y[:, 0:128]), (1, y[:, 128:256]), (2, p2), (4, y[:, 256:384]), (5, y[:, 384:512]), (6, pltpu.roll(p2, 64, 1))):
                rows[pl.ds(base + k, 512, stride=8), :] = piece
            xf = x.astype(F32)
            for g in range(0, 512, LANES):
                s_all = s_all + xf[:, g:g + LANES]
                if start + g < ifb:
                    s_face = s_face + xf[:, g:g + LANES]
    own = fold(s_all * jsum + s_face * fsum) - src_sum

    place_copy.wait()
    group = stage.shape[1]
    groups = n_dev // group
    lane8 = iota((8, LANES), 1)

    def gather(g, buf):
        for u in range(group):
            for k in range(CAP):
                at = pl.multiple_of(place_s[0, k * n_dev + g * group + u], 4)
                stage[buf, u, k * 4:k * 4 + 4, :] = rows[pl.ds(at, 4), :]

    def emit(g, buf, acc):
        for u in range(group):
            d = g * group + u
            p0, p1, p2 = [stage[buf, u, pl.ds(i, CAP, stride=4), :] for i in range(3)]
            low = jnp.where(lane8 < 64, p2[0:8], pltpu.roll(p2[16:24], 64, 1))
            high = jnp.where(lane8 < 64, p2[8:16], jnp.broadcast_to(numbers[pl.ds(d, 1), :], (8, LANES)))
            block = jnp.concatenate([p0[0:16], p1[0:16], p0[16:24], p1[16:24], low, high], axis=0).astype(BF16)
            send[d] = block
            q = block.astype(F32)
            acc = acc + (q[0:8] + q[8:16] + q[32:40])
        return acc

    gather(0, 0)

    def both(i, acc):
        gather(2 * i + 1, 1)
        acc = emit(2 * i, 0, acc)
        gather(jnp.minimum(2 * i + 2, groups - 1), 0)
        return emit(2 * i + 1, 1, acc)

    parts = out_sems.shape[0] - 1
    each = groups // 2 // parts
    acc = jnp.zeros((8, LANES), F32)
    outs = []
    for i in range(parts):
        acc = lax.fori_loop(i * each, (i + 1) * each, both, acc)
        at = pl.ds(i * (n_dev // parts), n_dev // parts)
        outs.append(pltpu.make_async_copy(send.at[at, pl.ds(0, 48)], send_hbm.at[at, pl.ds(0, 48)], out_sems.at[i]))
        outs[-1].start()
    mass = jnp.sum(own + jnp.where(lane8 < NODES, acc, 0.0), keepdims=True)
    m0 = mass.astype(BF16).astype(F32)
    m1 = (mass - m0).astype(BF16).astype(F32)
    m2 = mass - m0 - m1
    lane = iota((16, LANES), 1)
    add = jnp.where(lane == 112, m0, jnp.where(lane == 113, m1, jnp.where(lane == 114, m2, 0.0)))
    add = jnp.where(iota((16, LANES), 0) >= 8, add, 0.0).astype(BF16)

    for d in range(0, n_dev, 16):
        send[d:d + 16, 48:64, :] += add[None]
    outs.append(pltpu.make_async_copy(send.at[:, pl.ds(48, 16)], send_hbm.at[:, pl.ds(48, 16)], out_sems.at[parts]))
    outs[-1].start()
    for copy in outs:
        copy.wait()


def pack(cnt, owner, recv, slot, dblk, adj, met, src, jac, face, weights, n_dev, ifb=384):
    width, blocks = adj.shape
    n_rec = owner.shape[1]
    tiles = (2048, 2048)
    hbm = pl.BlockSpec(memory_space=pl.ANY)
    vmem = pl.BlockSpec(memory_space=pltpu.VMEM)
    return pl.pallas_call(
        functools.partial(pack_kernel, tiles, ifb),
        in_specs=[vmem] * 5 + [hbm] * 6,
        out_specs=hbm,
        out_shape=jax.ShapeDtypeStruct((n_dev, 64, LANES), BF16),
        scratch_shapes=[
            pltpu.VMEM((n_dev, 64, LANES), BF16),
            pltpu.VMEM((width, blocks), BF16),
            pltpu.VMEM((width, blocks), BF16),
            pltpu.VMEM((NODES, blocks), BF16),
            pltpu.VMEM((width, width), BF16),
            pltpu.VMEM((width, width), BF16),
            pltpu.VMEM((2, width, width), BF16),
            pltpu.VMEM((width, 640), BF16),
            pltpu.VMEM(((blocks + 1) * 8, LANES), F32),
            pltpu.VMEM((2, 4, CAP * 4, LANES), F32),
            pltpu.VMEM((1, CAP * n_dev), jnp.int32),
            pltpu.SMEM((1, CAP * n_dev), jnp.int32),
            pltpu.VMEM((n_dev, LANES), F32),
            pltpu.SemaphoreType.DMA((len(tiles), 2)),
            pltpu.SemaphoreType.DMA((4,)),
            pltpu.SemaphoreType.DMA((5,)),
            pltpu.SemaphoreType.DMA,
        ],
        compiler_params=pltpu.CompilerParams(vmem_limit_bytes=VMEM_LIMIT),
        cost_estimate=pl.CostEstimate(flops=2 * blocks * width * 2 * width, bytes_accessed=8 << 20, transcendentals=0),
        name="pack",
    )(cnt, owner, recv, slot, dblk, adj, met, src, jac, face, weights)


def face_out_kernel(adj_ref, met_ref, nbr_ref, out_ref):
    width, ifb = adj_ref.shape
    out_ref[0:width, :] = product(adj_ref[...], met_ref[...])
    nbr = nbr_ref[...].reshape(1, ifb)
    r = iota((16, ifb), 0)
    out_ref[width:width + 16, :] = jnp.where(r < 8, nbr >> 5, nbr & 31).astype(F32).astype(BF16)


def face_out(adj, met, nbr):
    width, _ = adj.shape
    ifb = nbr.shape[0]
    return pl.pallas_call(
        face_out_kernel,
        grid=(1,),
        in_specs=[
            pl.BlockSpec((width, ifb), lambda t: (0, 0)),
            pl.BlockSpec((width, ifb), lambda t: (0, 0)),
            pl.BlockSpec((ifb,), lambda t: (0,)),
        ],
        out_specs=pl.BlockSpec((width + 16, ifb), lambda t: (0, 0)),
        out_shape=jax.ShapeDtypeStruct((width + 16, ifb), BF16),
        compiler_params=pltpu.CompilerParams(vmem_limit_bytes=VMEM_LIMIT),
        name="face_out",
    )(adj, met, nbr)


WIDE = 6


def partial_kernel(me_ref, adj_ref, met_ref, src_ref, jac_ref, face_ref, *rest):
    got_refs, out_ref = rest[:-1], rest[-1]
    t = pl.program_id(0)
    width = adj_ref.shape[0]
    x = product(adj_ref[...], met_ref[...])
    out_ref[...] = dot(jac_ref[0], x, DOT00) - src_ref[...].astype(F32)

    @pl.when(t == 0)
    def _():
        ifb = got_refs[0].shape[1]
        acc = jnp.zeros((width, ifb), F32)
        for got_ref in got_refs:
            term = dot(face_ref[...], got_ref[0:width, :], DOT00)
            number = got_ref[width:width + 16, :].astype(F32)
            nbr = (number[0:1] * 32.0 + number[8:9]).astype(jnp.int32) - me_ref[0] * ifb
            hit = jnp.where(iota((ifb, ifb), 0) == nbr, 1.0, 0.0).astype(F32).astype(BF16)
            acc = acc + dot(term.astype(BF16), hit, DOT11)
        out_ref[:, 0:ifb] += acc


def partial_total(me, adj, met, src, jac, face, faces):
    width, blocks = adj.shape
    tile = 512
    col = lambda t: (0, t)
    return pl.pallas_call(
        partial_kernel,
        grid=(blocks // tile,),
        in_specs=[
            pl.BlockSpec(memory_space=pltpu.SMEM),
            pl.BlockSpec((width, tile), col),
            pl.BlockSpec((width, tile), col),
            pl.BlockSpec((width, tile), col),
            pl.BlockSpec((1, width, width), lambda t: (0, 0, 0)),
            pl.BlockSpec((width, width), lambda t: (0, 0)),
        ] + [pl.BlockSpec(faces[0].shape, lambda t: (0, 0))] * len(faces),
        out_specs=pl.BlockSpec((width, tile), col),
        out_shape=jax.ShapeDtypeStruct((width, WIDE * blocks), F32),
        compiler_params=pltpu.CompilerParams(vmem_limit_bytes=VMEM_LIMIT),
        cost_estimate=pl.CostEstimate(flops=2 * blocks * width * width, bytes_accessed=13 << 20, transcendentals=0),
        name="partial",
    )(me, adj, met, src, jac, face, *faces)


ROOM = 192
BUCKET = 256


def unpack_kernel(
    scale, got, part_hbm, out_hbm, mass_ref,
    part, out, q, stage, numbers, bucket, rank, low, place_v, place_s, ids, in_sem, out_sems, sem,
):
    n_dev = got.shape[0]
    width, blocks = out.shape
    n_buckets = blocks // BUCKET
    part_in = pltpu.make_async_copy(part_hbm.at[:, pl.ds(0, blocks)], part, in_sem)
    part_in.start()
    q[0:8, :] = jnp.zeros((8, LANES), F32)

    def number(s, _):
        numbers[pl.ds(s, 1), :] = got[s, 48:64, :].astype(F32)[8:9]
        return 0

    lax.fori_loop(0, n_dev, number, 0, unroll=16)

    lane = iota((n_dev, LANES), 1)
    nums = numbers[...]
    mass_ref[0, 0] = jnp.sum(jnp.where((lane >= 112) & (lane < 115), nums, 0.0)) * scale
    nums = nums.T
    block = (nums[64:64 + CAP] * 32.0 + nums[64 + CAP:64 + 2 * CAP]).astype(jnp.int32) - 1
    bucket[...] = block >> 8
    low[...] = (block & 255) + 1

    def hits(k):
        return jnp.where(iota((n_buckets, LANES), 0) == bucket[k:k + 1, :], 1.0, 0.0).astype(F32)

    upper = (iota((LANES, LANES), 0) < iota((LANES, LANES), 1)).astype(BF16)
    hit = [hits(k) for k in range(CAP)]
    before = dot(jnp.concatenate(hit, axis=0).astype(BF16), upper, DOT10)
    carry = jnp.zeros((n_buckets, 1), F32)
    for k in range(CAP):
        at = k * n_buckets
        rank[k:k + 1, :] = jnp.sum(hit[k] * (before[at:at + n_buckets] + carry), axis=0, keepdims=True).astype(jnp.int32)
        carry = carry + jnp.sum(hit[k], axis=1, keepdims=True)
    rounds = (jnp.max(carry).astype(jnp.int32) + ROOM - 1) // ROOM

    def choose(turn):
        table = jnp.zeros((n_buckets, 2 * ROOM), F32)
        inside = jnp.zeros((ROOM, n_buckets), F32)
        wide = lambda ref, k: jnp.concatenate([ref[k:k + 1, :], ref[k + 1:k + 2, :]], axis=1)
        for k in range(0, CAP, 2):
            here = iota((ROOM, 2 * LANES), 0) == wide(rank, k) - turn * ROOM
            l = iota((1, 2 * LANES), 1)
            record = (l & (LANES - 1)) * CAP + (l >> 7) + k + 2
            pair = jnp.concatenate([hits(k), hits(k + 1)], axis=1).astype(BF16)
            mark = lambda v: jnp.where(here, v, 0).astype(F32).astype(BF16)
            table = table + dot(pair, jnp.concatenate([mark(record >> 6), mark(record & 63)], axis=0), DOT11)
            inside = inside + dot(mark(wide(low, k)), pair, DOT11)
        place_v[:, 0:ROOM] = (table[:, 0:ROOM] * 256.0 + table[:, ROOM:] * 4.0).astype(jnp.int32)
        ids[:, 0:n_buckets] = inside.astype(jnp.int32) - 1
        return pltpu.make_async_copy(place_v, place_s, sem)

    def gather(b, buf):
        for p in range(ROOM):
            at = pl.multiple_of(place_s[b, p], 4)
            stage[buf, p * 4:p * 4 + 4, :] = q[pl.ds(at, 4), :]

    def added(b, buf):
        rows = jnp.concatenate([stage[buf, pl.ds(i, ROOM, stride=4), :].astype(BF16) for i in range(3)], axis=1)
        mine = jnp.sum(jnp.where(iota((ROOM, n_buckets), 1) == b, ids[:, 0:n_buckets], 0), axis=1, keepdims=True)
        mark = jnp.where(iota((ROOM, BUCKET), 1) == mine, 1.0, 0.0).astype(F32).astype(BF16)
        at = pl.ds(pl.multiple_of(b * BUCKET, BUCKET), BUCKET)
        return part[:, at] + dot(rows, mark, DOT00)[0:width]

    def take(s, _):
        g = got[s].astype(F32)
        at = (s * CAP + 2) * 4
        q[pl.ds(at, 16, stride=4), :] = g[0:16]
        q[pl.ds(at + 1, 16, stride=4), :] = g[16:32]
        q[pl.ds(at + 2, 16, stride=4), :] = g[48:64]
        q[pl.ds(at + 64, 8, stride=4), :] = g[32:40]
        q[pl.ds(at + 65, 8, stride=4), :] = g[40:48]
        q[pl.ds(at + 66, 8, stride=4), :] = pltpu.roll(g[48:56], 64, 1)
        return 0

    place_copy = choose(0)
    place_copy.start()
    lax.fori_loop(0, n_dev, take, 0, unroll=8)
    part_in.wait()
    place_copy.wait()

    def more(turn, _):
        copy = choose(turn)
        copy.start()
        copy.wait()

        def one(b, _):
            gather(b, 0)
            at = pl.ds(pl.multiple_of(b * BUCKET, BUCKET), BUCKET)
            part[:, at] = added(b, 0)
            return 0

        return lax.fori_loop(0, n_buckets, one, 0)

    @pl.when(rounds > 1)
    def _():
        lax.fori_loop(1, rounds, more, 0)
        again = choose(0)
        again.start()
        again.wait()

    def out_copy(i):
        at = pl.ds(pl.multiple_of(i * 2 * BUCKET, 2 * BUCKET), 2 * BUCKET)
        return pltpu.make_async_copy(out.at[:, at], out_hbm.at[:, at], out_sems.at[i])

    def put(b, buf):
        at = pl.ds(pl.multiple_of(b * BUCKET, BUCKET), BUCKET)
        out[:, at] = added(b, buf).astype(BF16)

    gather(0, 0)

    def both(i, _):
        gather(2 * i + 1, 1)
        put(2 * i, 0)
        gather(jnp.minimum(2 * i + 2, n_buckets - 1), 0)
        put(2 * i + 1, 1)
        out_copy(i).start()
        return 0

    lax.fori_loop(0, n_buckets // 2, both, 0)

    def finish(i, _):
        out_copy(i).wait()
        return 0

    lax.fori_loop(0, n_buckets // 2, finish, 0)


def unpack(got, part, blocks, scale):
    width = part.shape[0]
    n_dev = got.shape[0]
    n_buckets = blocks // BUCKET
    hbm = pl.BlockSpec(memory_space=pl.ANY)
    return pl.pallas_call(
        functools.partial(unpack_kernel, scale),
        in_specs=[pl.BlockSpec(memory_space=pltpu.VMEM), hbm],
        out_specs=[hbm, pl.BlockSpec(memory_space=pltpu.SMEM)],
        out_shape=[
            jax.ShapeDtypeStruct((width, blocks), BF16),
            jax.ShapeDtypeStruct((1, 1), F32),
        ],
        scratch_shapes=[
            pltpu.VMEM((width, blocks), F32),
            pltpu.VMEM((width, blocks), BF16),
            pltpu.VMEM(((n_dev * CAP + 2) * 4, LANES), F32),
            pltpu.VMEM((2, ROOM * 4, LANES), F32),
            pltpu.VMEM((n_dev, LANES), F32),
            pltpu.VMEM((CAP, n_dev), jnp.int32),
            pltpu.VMEM((CAP, n_dev), jnp.int32),
            pltpu.VMEM((CAP, n_dev), jnp.int32),
            pltpu.VMEM((n_buckets, 256), jnp.int32),
            pltpu.SMEM((n_buckets, 256), jnp.int32),
            pltpu.VMEM((ROOM, LANES), jnp.int32),
            pltpu.SemaphoreType.DMA,
            pltpu.SemaphoreType.DMA((n_buckets // 2,)),
            pltpu.SemaphoreType.DMA,
        ],
        compiler_params=pltpu.CompilerParams(vmem_limit_bytes=32 * 1024 * 1024),
        cost_estimate=pl.CostEstimate(flops=2 * blocks * width * BUCKET, bytes_accessed=10 << 20, transcendentals=0),
        name="unpack",
    )(got, part)


def shards(
    adjoint, metric, comp_jac, face_jac, donor_weights, source, face_nbr,
    receiver_block, donor_owner, donor_block, donor_slot, fringe_count,
):
    blocks, width = adjoint.shape
    n_dev = lax.axis_size("comp") * lax.axis_size("blk")
    adj, met, src = adjoint.T, metric.T, source.T
    row = lambda a: a.reshape(1, -1)
    own = face_out(adj, met, face_nbr)
    n_comp = lax.axis_size("comp")
    faces = [own] + [
        lax.ppermute(own, "comp", [(i, (i + k) % n_comp) for i in range(n_comp)]) for k in range(1, n_comp)
    ]
    send = pack(
        fringe_count, row(donor_owner), row(receiver_block), row(donor_slot), row(donor_block),
        adj, met, src, comp_jac, face_jac, donor_weights, n_dev,
    )
    send, *faces = lax.optimization_barrier((send, *faces))
    got = lax.all_to_all(send, ("comp", "blk"), split_axis=0, concat_axis=0, tiled=True)
    me = lax.axis_index("comp").astype(jnp.int32).reshape(1)
    part = partial_total(me, adj, met, src, comp_jac, face_jac, faces)
    out, mass = unpack(got, part, blocks, 1.0 / float(blocks * n_dev * NODES) ** 0.5)
    return out.T, mass.reshape(())


def solution(mesh):
    both = ("comp", "blk")
    placed = (
        P(both, None), P(both, None), P("comp", None, None), P(), P(), P(both, None),
        P(both), P(both), P(both, None), P(both), P(both), P(both),
    )
    return jax.shard_map(
        shards, mesh=mesh, in_specs=placed, out_specs=(P(both, None), P()), check_vma=False,
    )
```

```python
import functools

import jax
import jax.numpy as jnp
from jax import lax
from jax.experimental import pallas as pl
from jax.experimental.pallas import tpu as pltpu
from jax.sharding import PartitionSpec as P

NODES = 64
CAP = 24
LANES = 128
DOT00 = (((0,), (0,)), ((), ()))
DOT11 = (((1,), (1,)), ((), ()))
DOT10 = (((1,), (0,)), ((), ()))
F32 = jnp.float32
BF16 = jnp.bfloat16
VMEM_LIMIT = 60 * 1024 * 1024


def dot(a, b, dims):
    return lax.dot_general(a, b, dims, preferred_element_type=F32)


def iota(shape, axis):
    return lax.broadcasted_iota(jnp.int32, shape, axis)


def product(a, b):
    return (a.astype(F32) * b.astype(F32)).astype(BF16)


def pack_kernel(
    tiles, ifb, cnt_ref, owner_ref, recv_ref, slot_ref, dblk_ref, adj_hbm, met_hbm, src_hbm, jac_hbm, face_hbm, w_hbm,
    send_hbm, send, adj, met, src, jac, face, w, wcat, rows, stage, place_v, place_s, numbers, sems, late_sems, out_sems, sem,
):
    n_dev = send.shape[0]
    n_rec = owner_ref.shape[1]

    w_copy = pltpu.make_async_copy(w_hbm, w, late_sems.at[0])
    w_copy.start()
    loads = []
    first = 0
    for t, size in enumerate(tiles):
        at = pl.ds(first, size)
        loads.append((
            first, size,
            pltpu.make_async_copy(adj_hbm.at[:, at], adj.at[:, at], sems.at[t, 0]),
            pltpu.make_async_copy(met_hbm.at[:, at], met.at[:, at], sems.at[t, 1]),
        ))
        first += size
    late = [
        pltpu.make_async_copy(src_hbm.at[pl.ds(0, NODES), :], src, late_sems.at[1]),
        pltpu.make_async_copy(jac_hbm.at[0], jac, late_sems.at[2]),
        pltpu.make_async_copy(face_hbm, face, late_sems.at[3]),
    ]
    for t, (_, _, one, two) in enumerate(loads):
        one.start()
        two.start()
        if t == 0:
            for copy in late:
                copy.start()

    rows[0:8, :] = jnp.zeros((8, LANES), F32)
    cnt = cnt_ref[...].reshape(1, 1)
    step = 256
    upper = (iota((step, step), 0) < iota((step, step), 1)).astype(BF16)
    j = iota((LANES, step), 0)
    krow = jnp.where(j < 48, j % CAP, jnp.where(j < 64, -1, jnp.where(j < 112, (j - 64) % CAP, -1)))
    carry = jnp.zeros((n_dev, 1), F32)
    table = jnp.zeros((n_dev, LANES), F32)
    table_t = jnp.zeros((LANES, n_dev), F32)
    for c in range(n_rec // step):
        at = slice(c * step, (c + 1) * step)
        live = (iota((1, step), 1) + c * step) < cnt
        hit = (iota((n_dev, step), 0) == owner_ref[:, at]) & live
        a = jnp.where(hit, 1.0, 0.0).astype(F32)
        ab = a.astype(BF16)
        before = dot(ab, upper, DOT10) + carry
        rank = jnp.sum(a * before, axis=0, keepdims=True).astype(jnp.int32)
        carry = carry + jnp.sum(a, axis=1, keepdims=True)
        tag = dblk_ref[:, at] + 1
        at_row = recv_ref[:, at] * 2 + slot_ref[:, at] + 2
        feature = jnp.where(j < 24, at_row >> 7, jnp.where(j < 48, at_row & 127, jnp.where(j < 88, tag >> 5, tag & 31)))
        z = jnp.where(krow == rank, feature, 0).astype(F32).astype(BF16)
        table = table + dot(ab, z, DOT11)
        table_t = table_t + dot(z, ab, DOT11)
    numbers[...] = table
    place = (table_t[0:24] * 512.0 + table_t[24:48] * 4.0).astype(jnp.int32)
    for k in range(CAP):
        place_v[0:1, k * n_dev:(k + 1) * n_dev] = place[k:k + 1]
    place_copy = pltpu.make_async_copy(place_v, place_s, sem)
    place_copy.start()

    w_copy.wait()
    wcat[:, 0:256] = w[0, :, 0:256]
    wcat[:, 256:512] = w[1, :, 0:256]
    wcat[:, 512:640] = jnp.concatenate([w[0, :, 256:320], w[1, :, 256:320]], axis=1)
    s_all = jnp.zeros((adj.shape[0], LANES), F32)
    s_face = jnp.zeros((adj.shape[0], LANES), F32)
    fold = lambda v: jnp.sum(v.reshape(-1, 8, LANES), axis=0)
    for first, size, one, two in loads:
        one.wait()
        two.wait()
        if first == 0:
            for copy in late:
                copy.wait()
            jsum = jnp.sum(jac[:, 0:NODES].astype(F32), axis=1, keepdims=True)
            fsum = jnp.sum(face[:, 0:NODES].astype(F32), axis=1, keepdims=True)
            src_sum = jnp.zeros((8, LANES), F32)
            for g in range(0, src.shape[1], LANES):
                src_sum = src_sum + fold(src[:, g:g + LANES].astype(F32))
        for start in range(first, first + size, 512):
            at = slice(start, start + 512)
            x = product(adj[:, at], met[:, at])
            y = dot(x, wcat[...], DOT00)
            base = (start + 1) * 8
            p2 = y[:, 512:640]
            for k, piece in ((0, y[:, 0:128]), (1, y[:, 128:256]), (2, p2), (4, y[:, 256:384]), (5, y[:, 384:512]), (6, pltpu.roll(p2, 64, 1))):
                rows[pl.ds(base + k, 512, stride=8), :] = piece
            xf = x.astype(F32)
            for g in range(0, 512, LANES):
                s_all = s_all + xf[:, g:g + LANES]
                if start + g < ifb:
                    s_face = s_face + xf[:, g:g + LANES]
    own = fold(s_all * jsum + s_face * fsum) - src_sum

    place_copy.wait()
    group = stage.shape[1]
    groups = n_dev // group
    lane8 = iota((8, LANES), 1)

    def gather(g, buf):
        for u in range(group):
            for k in range(CAP):
                at = pl.multiple_of(place_s[0, k * n_dev + g * group + u], 4)
                stage[buf, u, k * 4:k * 4 + 4, :] = rows[pl.ds(at, 4), :]

    def emit(g, buf, acc):
        for u in range(group):
            d = g * group + u
            p0, p1, p2 = [stage[buf, u, pl.ds(i, CAP, stride=4), :] for i in range(3)]
            low = jnp.where(lane8 < 64, p2[0:8], pltpu.roll(p2[16:24], 64, 1))
            high = jnp.where(lane8 < 64, p2[8:16], jnp.broadcast_to(numbers[pl.ds(d, 1), :], (8, LANES)))
            block = jnp.concatenate([p0[0:16], p1[0:16], p0[16:24], p1[16:24], low, high], axis=0).astype(BF16)
            send[d] = block
            q = block.astype(F32)
            acc = acc + (q[0:8] + q[8:16] + q[32:40])
        return acc

    gather(0, 0)

    parts = out_sems.shape[0] - 1
    each = groups // parts
    acc = jnp.zeros((8, LANES), F32)
    outs = []
    for i in range(parts):
        for g in range(i * each, (i + 1) * each):
            if g + 1 < groups:
                gather(g + 1, (g + 1) % 2)
            acc = emit(g, g % 2, acc)
        at = pl.ds(i * (n_dev // parts), n_dev // parts)
        outs.append(pltpu.make_async_copy(send.at[at, pl.ds(0, 48)], send_hbm.at[at, pl.ds(0, 48)], out_sems.at[i]))
        outs[-1].start()
    mass = jnp.sum(own + jnp.where(lane8 < NODES, acc, 0.0), keepdims=True)
    m0 = mass.astype(BF16).astype(F32)
    m1 = (mass - m0).astype(BF16).astype(F32)
    m2 = mass - m0 - m1
    lane = iota((16, LANES), 1)
    add = jnp.where(lane == 112, m0, jnp.where(lane == 113, m1, jnp.where(lane == 114, m2, 0.0)))
    add = jnp.where(iota((16, LANES), 0) >= 8, add, 0.0).astype(BF16)

    for d in range(0, n_dev, 16):
        send[d:d + 16, 48:64, :] += add[None]
    outs.append(pltpu.make_async_copy(send.at[:, pl.ds(48, 16)], send_hbm.at[:, pl.ds(48, 16)], out_sems.at[parts]))
    outs[-1].start()
    for copy in outs:
        copy.wait()


def pack(cnt, owner, recv, slot, dblk, adj, met, src, jac, face, weights, n_dev, ifb=384):
    width, blocks = adj.shape
    n_rec = owner.shape[1]
    tiles = (2048, 2048)
    hbm = pl.BlockSpec(memory_space=pl.ANY)
    vmem = pl.BlockSpec(memory_space=pltpu.VMEM)
    return pl.pallas_call(
        functools.partial(pack_kernel, tiles, ifb),
        in_specs=[vmem] * 5 + [hbm] * 6,
        out_specs=hbm,
        out_shape=jax.ShapeDtypeStruct((n_dev, 64, LANES), BF16),
        scratch_shapes=[
            pltpu.VMEM((n_dev, 64, LANES), BF16),
            pltpu.VMEM((width, blocks), BF16),
            pltpu.VMEM((width, blocks), BF16),
            pltpu.VMEM((NODES, blocks), BF16),
            pltpu.VMEM((width, width), BF16),
            pltpu.VMEM((width, width), BF16),
            pltpu.VMEM((2, width, width), BF16),
            pltpu.VMEM((width, 640), BF16),
            pltpu.VMEM(((blocks + 1) * 8, LANES), F32),
            pltpu.VMEM((2, 4, CAP * 4, LANES), F32),
            pltpu.VMEM((1, CAP * n_dev), jnp.int32),
            pltpu.SMEM((1, CAP * n_dev), jnp.int32),
            pltpu.VMEM((n_dev, LANES), F32),
            pltpu.SemaphoreType.DMA((len(tiles), 2)),
            pltpu.SemaphoreType.DMA((4,)),
            pltpu.SemaphoreType.DMA((5,)),
            pltpu.SemaphoreType.DMA,
        ],
        compiler_params=pltpu.CompilerParams(vmem_limit_bytes=VMEM_LIMIT),
        cost_estimate=pl.CostEstimate(flops=2 * blocks * width * 2 * width, bytes_accessed=8 << 20, transcendentals=0),
        name="pack",
    )(cnt, owner, recv, slot, dblk, adj, met, src, jac, face, weights)


def face_out_kernel(adj_ref, met_ref, nbr_ref, out_ref):
    width, ifb = adj_ref.shape
    out_ref[0:width, :] = product(adj_ref[...], met_ref[...])
    nbr = nbr_ref[...].reshape(1, ifb)
    r = iota((16, ifb), 0)
    out_ref[width:width + 16, :] = jnp.where(r < 8, nbr >> 5, nbr & 31).astype(F32).astype(BF16)


def face_out(adj, met, nbr):
    width, _ = adj.shape
    ifb = nbr.shape[0]
    return pl.pallas_call(
        face_out_kernel,
        grid=(1,),
        in_specs=[
            pl.BlockSpec((width, ifb), lambda t: (0, 0)),
            pl.BlockSpec((width, ifb), lambda t: (0, 0)),
            pl.BlockSpec((ifb,), lambda t: (0,)),
        ],
        out_specs=pl.BlockSpec((width + 16, ifb), lambda t: (0, 0)),
        out_shape=jax.ShapeDtypeStruct((width + 16, ifb), BF16),
        compiler_params=pltpu.CompilerParams(vmem_limit_bytes=VMEM_LIMIT),
        name="face_out",
    )(adj, met, nbr)


WIDE = 6


def partial_kernel(me_ref, adj_ref, met_ref, src_ref, jac_ref, face_ref, *rest):
    got_refs, out_ref = rest[:-1], rest[-1]
    t = pl.program_id(0)
    width = adj_ref.shape[0]
    x = product(adj_ref[...], met_ref[...])
    out_ref[...] = dot(jac_ref[0], x, DOT00) - src_ref[...].astype(F32)

    @pl.when(t == 0)
    def _():
        ifb = got_refs[0].shape[1]
        acc = jnp.zeros((width, ifb), F32)
        for got_ref in got_refs:
            term = dot(face_ref[...], got_ref[0:width, :], DOT00)
            number = got_ref[width:width + 16, :].astype(F32)
            nbr = (number[0:1] * 32.0 + number[8:9]).astype(jnp.int32) - me_ref[0] * ifb
            hit = jnp.where(iota((ifb, ifb), 0) == nbr, 1.0, 0.0).astype(F32).astype(BF16)
            acc = acc + dot(term.astype(BF16), hit, DOT11)
        out_ref[:, 0:ifb] += acc


def partial_total(me, adj, met, src, jac, face, faces):
    width, blocks = adj.shape
    tile = 512
    col = lambda t: (0, t)
    return pl.pallas_call(
        partial_kernel,
        grid=(blocks // tile,),
        in_specs=[
            pl.BlockSpec(memory_space=pltpu.SMEM),
            pl.BlockSpec((width, tile), col),
            pl.BlockSpec((width, tile), col),
            pl.BlockSpec((width, tile), col),
            pl.BlockSpec((1, width, width), lambda t: (0, 0, 0)),
            pl.BlockSpec((width, width), lambda t: (0, 0)),
        ] + [pl.BlockSpec(faces[0].shape, lambda t: (0, 0))] * len(faces),
        out_specs=pl.BlockSpec((width, tile), col),
        out_shape=jax.ShapeDtypeStruct((width, WIDE * blocks), F32),
        compiler_params=pltpu.CompilerParams(vmem_limit_bytes=VMEM_LIMIT),
        cost_estimate=pl.CostEstimate(flops=2 * blocks * width * width, bytes_accessed=13 << 20, transcendentals=0),
        name="partial",
    )(me, adj, met, src, jac, face, *faces)


ROOM = 192
BUCKET = 256


def unpack_kernel(
    scale, got, part_hbm, out_hbm, mass_ref,
    part, out, q, stage, numbers, bucket, rank, low, place_v, place_s, ids, in_sem, out_sems, sem,
):
    n_dev = got.shape[0]
    width, blocks = out.shape
    n_buckets = blocks // BUCKET
    part_in = pltpu.make_async_copy(part_hbm.at[:, pl.ds(0, blocks)], part, in_sem)
    part_in.start()
    q[0:8, :] = jnp.zeros((8, LANES), F32)

    def number(s, _):
        numbers[pl.ds(s, 1), :] = got[s, 48:64, :].astype(F32)[8:9]
        return 0

    lax.fori_loop(0, n_dev, number, 0, unroll=16)

    lane = iota((n_dev, LANES), 1)
    nums = numbers[...]
    mass_ref[0, 0] = jnp.sum(jnp.where((lane >= 112) & (lane < 115), nums, 0.0)) * scale
    nums = nums.T
    block = (nums[64:64 + CAP] * 32.0 + nums[64 + CAP:64 + 2 * CAP]).astype(jnp.int32) - 1
    bucket[...] = block >> 8
    low[...] = (block & 255) + 1

    def hits(k):
        return jnp.where(iota((n_buckets, LANES), 0) == bucket[k:k + 1, :], 1.0, 0.0).astype(F32)

    upper = (iota((LANES, LANES), 0) < iota((LANES, LANES), 1)).astype(BF16)
    hit = [hits(k) for k in range(CAP)]
    before = dot(jnp.concatenate(hit, axis=0).astype(BF16), upper, DOT10)
    carry = jnp.zeros((n_buckets, 1), F32)
    for k in range(CAP):
        at = k * n_buckets
        rank[k:k + 1, :] = jnp.sum(hit[k] * (before[at:at + n_buckets] + carry), axis=0, keepdims=True).astype(jnp.int32)
        carry = carry + jnp.sum(hit[k], axis=1, keepdims=True)
    rounds = (jnp.max(carry).astype(jnp.int32) + ROOM - 1) // ROOM

    def choose(turn):
        table = jnp.zeros((n_buckets, 2 * ROOM), F32)
        inside = jnp.zeros((ROOM, n_buckets), F32)
        wide = lambda ref, k: jnp.concatenate([ref[k:k + 1, :], ref[k + 1:k + 2, :]], axis=1)
        for k in range(0, CAP, 2):
            here = iota((ROOM, 2 * LANES), 0) == wide(rank, k) - turn * ROOM
            l = iota((1, 2 * LANES), 1)
            record = (l & (LANES - 1)) * CAP + (l >> 7) + k + 2
            pair = jnp.concatenate([hits(k), hits(k + 1)], axis=1).astype(BF16)
            mark = lambda v: jnp.where(here, v, 0).astype(F32).astype(BF16)
            table = table + dot(pair, jnp.concatenate([mark(record >> 6), mark(record & 63)], axis=0), DOT11)
            inside = inside + dot(mark(wide(low, k)), pair, DOT11)
        place_v[:, 0:ROOM] = (table[:, 0:ROOM] * 256.0 + table[:, ROOM:] * 4.0).astype(jnp.int32)
        ids[:, 0:n_buckets] = inside.astype(jnp.int32) - 1
        return pltpu.make_async_copy(place_v, place_s, sem)

    def gather(b, buf):
        for p in range(ROOM):
            at = pl.multiple_of(place_s[b, p], 4)
            stage[buf, p * 4:p * 4 + 4, :] = q[pl.ds(at, 4), :]

    def added(b, buf):
        rows = jnp.concatenate([stage[buf, pl.ds(i, ROOM, stride=4), :].astype(BF16) for i in range(3)], axis=1)
        if isinstance(b, int):
            mine = ids[:, b:b + 1]
        else:
            mine = jnp.sum(jnp.where(iota((ROOM, n_buckets), 1) == b, ids[:, 0:n_buckets], 0), axis=1, keepdims=True)
        mark = jnp.where(iota((ROOM, BUCKET), 1) == mine, 1.0, 0.0).astype(F32).astype(BF16)
        at = pl.ds(b * BUCKET if isinstance(b, int) else pl.multiple_of(b * BUCKET, BUCKET), BUCKET)
        return part[:, at] + dot(rows, mark, DOT00)[0:width]

    def take(s, _):
        g = got[s].astype(F32)
        at = (s * CAP + 2) * 4
        q[pl.ds(at, 16, stride=4), :] = g[0:16]
        q[pl.ds(at + 1, 16, stride=4), :] = g[16:32]
        q[pl.ds(at + 2, 16, stride=4), :] = g[48:64]
        q[pl.ds(at + 64, 8, stride=4), :] = g[32:40]
        q[pl.ds(at + 65, 8, stride=4), :] = g[40:48]
        q[pl.ds(at + 66, 8, stride=4), :] = pltpu.roll(g[48:56], 64, 1)
        return 0

    place_copy = choose(0)
    place_copy.start()
    lax.fori_loop(0, n_dev, take, 0, unroll=16)
    part_in.wait()
    place_copy.wait()

    def more(turn, _):
        copy = choose(turn)
        copy.start()
        copy.wait()

        def one(b, _):
            gather(b, 0)
            at = pl.ds(pl.multiple_of(b * BUCKET, BUCKET), BUCKET)
            part[:, at] = added(b, 0)
            return 0

        return lax.fori_loop(0, n_buckets, one, 0)

    @pl.when(rounds > 1)
    def _():
        lax.fori_loop(1, rounds, more, 0)
        again = choose(0)
        again.start()
        again.wait()

    def out_copy(i):
        at = pl.ds(i * 2 * BUCKET, 2 * BUCKET)
        return pltpu.make_async_copy(out.at[:, at], out_hbm.at[:, at], out_sems.at[i])

    def put(b, buf):
        at = pl.ds(b * BUCKET, BUCKET)
        out[:, at] = added(b, buf).astype(BF16)

    gather(0, 0)

    for b in range(n_buckets):
        if b + 1 < n_buckets:
            gather(b + 1, (b + 1) % 2)
        put(b, b % 2)
        if b % 2:
            out_copy(b // 2).start()
    for i in range(n_buckets // 2):
        out_copy(i).wait()


def unpack(got, part, blocks, scale):
    width = part.shape[0]
    n_dev = got.shape[0]
    n_buckets = blocks // BUCKET
    hbm = pl.BlockSpec(memory_space=pl.ANY)
    return pl.pallas_call(
        functools.partial(unpack_kernel, scale),
        in_specs=[pl.BlockSpec(memory_space=pltpu.VMEM), hbm],
        out_specs=[hbm, pl.BlockSpec(memory_space=pltpu.SMEM)],
        out_shape=[
            jax.ShapeDtypeStruct((width, blocks), BF16),
            jax.ShapeDtypeStruct((1, 1), F32),
        ],
        scratch_shapes=[
            pltpu.VMEM((width, blocks), F32),
            pltpu.VMEM((width, blocks), BF16),
            pltpu.VMEM(((n_dev * CAP + 2) * 4, LANES), F32),
            pltpu.VMEM((2, ROOM * 4, LANES), F32),
            pltpu.VMEM((n_dev, LANES), F32),
            pltpu.VMEM((CAP, n_dev), jnp.int32),
            pltpu.VMEM((CAP, n_dev), jnp.int32),
            pltpu.VMEM((CAP, n_dev), jnp.int32),
            pltpu.VMEM((n_buckets, 256), jnp.int32),
            pltpu.SMEM((n_buckets, 256), jnp.int32),
            pltpu.VMEM((ROOM, LANES), jnp.int32),
            pltpu.SemaphoreType.DMA,
            pltpu.SemaphoreType.DMA((n_buckets // 2,)),
            pltpu.SemaphoreType.DMA,
        ],
        compiler_params=pltpu.CompilerParams(vmem_limit_bytes=32 * 1024 * 1024),
        cost_estimate=pl.CostEstimate(flops=2 * blocks * width * BUCKET, bytes_accessed=10 << 20, transcendentals=0),
        name="unpack",
    )(got, part)


def shards(
    adjoint, metric, comp_jac, face_jac, donor_weights, source, face_nbr,
    receiver_block, donor_owner, donor_block, donor_slot, fringe_count,
):
    blocks, width = adjoint.shape
    n_dev = lax.axis_size("comp") * lax.axis_size("blk")
    adj, met, src = adjoint.T, metric.T, source.T
    row = lambda a: a.reshape(1, -1)
    own = face_out(adj, met, face_nbr)
    n_comp = lax.axis_size("comp")
    faces = [own] + [
        lax.ppermute(own, "comp", [(i, (i + k) % n_comp) for i in range(n_comp)]) for k in range(1, n_comp)
    ]
    send = pack(
        fringe_count, row(donor_owner), row(receiver_block), row(donor_slot), row(donor_block),
        adj, met, src, comp_jac, face_jac, donor_weights, n_dev,
    )
    send, *faces = lax.optimization_barrier((send, *faces))
    got = lax.all_to_all(send, ("comp", "blk"), split_axis=0, concat_axis=0, tiled=True)
    me = lax.axis_index("comp").astype(jnp.int32).reshape(1)
    part = partial_total(me, adj, met, src, comp_jac, face_jac, faces)
    out, mass = unpack(got, part, blocks, 1.0 / float(blocks * n_dev * NODES) ** 0.5)
    return out.T, mass.reshape(())


def solution(mesh):
    both = ("comp", "blk")
    placed = (
        P(both, None), P(both, None), P("comp", None, None), P(), P(), P(both, None),
        P(both), P(both), P(both, None), P(both), P(both), P(both),
    )
    return jax.shard_map(
        shards, mesh=mesh, in_specs=placed, out_specs=(P(both, None), P()), check_vma=False,
    )
```
